128 devices in a mesh: fsdp: 32 (over z_lo, x, y), dp: 4 (over z_hi, core).
Axes of the slice: x: 4, y: 4, z: 4 (z_hi: 2, z_lo: 2; z = z_hi * 2 + z_lo), core: 2. Of those that a mesh axis runs over, the one named last changes fastest.
Arguments:
- acts: bfloat16 [65536, 8192], P(('fsdp', 'dp')), may hold values from -60 to 60
- cotangent: bfloat16 [65536, 1024], P(('fsdp', 'dp')), may hold values from -6 to 6
- master: float32 [8192, 1024], P(('fsdp', 'dp')), may hold values from -0.12 to 0.12
- moment1: float32 [8192, 1024], P(('fsdp', 'dp')), may hold values from -0.000103580095 to 0.000103580095
- moment2: float32 [8192, 1024], P(('fsdp', 'dp')), may hold values from 1.1920929e-09 to 1.1920929e-08
- hidden_in: bfloat16 [4, 4, 32, 32, 1024], P(None, 'dp', 'fsdp'), may hold values from -6 to 6
- k_cache: bfloat16 [4, 32, 32, 512, 128], P('dp', 'fsdp'), may hold values from -8 to 8
- v_cache: bfloat16 [4, 32, 32, 512, 128], P('dp', 'fsdp'), may hold values from -6 to 6
- k_new: bfloat16 [4, 4, 32, 32, 128], P(None, 'dp', 'fsdp'), may hold values from -15 to 15
- queries: bfloat16 [4, 4, 32, 32, 1024], P(None, 'dp', 'fsdp'), may hold values from -200 to 200
- cache_len: int32 [4, 4, 32], P('dp'), may hold values from 64 to 508, as said below
Outputs:
- new_master: float32 [8192, 1024], P(('fsdp', 'dp'))
- attn_out: bfloat16 [4, 4, 32, 32, 1024], P(None, 'dp', 'fsdp')
The draws below stay inside these ranges and needn't reach their ends.
Inputs may be any that keep to these rules, and one draw needn't show every extreme that they name: `cache_len`: every sequence has between 64 and 508 filled slots; the first sequence of each replica has exactly 508.
All inputs are finite; a program needn't handle non-finite values.
Results may differ from the reference program's by a relative error of at most 0.0055.
Values may be sent and summed in bfloat16 or wider, within the bound.
A program may use at most 128 MiB of HBM per device.

```python
import jax
import jax.numpy as jnp
from jax import lax

D = 8192
KVH = 8
HD = 128
GQ = 8
ROWS = 32
CTX = 512
STEPS = 4
KVD = 1024
TOKENS = 65536
REPL = 4
N_FSDP = 32
N_DP = 4


def draw_acts(key, part):
    key = jax.random.fold_in(key, 11)
    keys = jax.random.split(key, 3)
    index = jnp.arange(TOKENS, dtype=jnp.float32)[:, None]
    rise = 3.0 ** (index / TOKENS)
    rowsc = jnp.exp(jax.random.uniform(keys[1], (TOKENS, 1), jnp.float32, 0.0, 2.3))
    colsc = jnp.exp(jax.random.uniform(keys[2], (1, D), jnp.float32, 0.0, 2.3))
    base = jax.random.normal(keys[0], (TOKENS, D), jnp.float32)
    vals = jnp.clip(0.25 * base * rise * rowsc * colsc, -60.0, 60.0)
    return vals.astype(jnp.bfloat16)


def draw_master(key, part):
    key = jax.random.fold_in(key, 51)
    vals = 0.02 * jnp.clip(jax.random.normal(key, (D, KVD), jnp.float32), -6.0, 6.0)
    return vals.astype(jnp.float32)


def draw_moment1(key, part):
    key = jax.random.fold_in(key, 53)
    unit = 0.05 * (D * KVD) ** (-0.5)
    vals = unit * jnp.clip(jax.random.normal(key, (D, KVD), jnp.float32), -6.0, 6.0)
    return vals.astype(jnp.float32)


def draw_moment2(key, part):
    key = jax.random.fold_in(key, 57)
    unit = (D * KVD) ** (-1.0)
    expo = jax.random.uniform(key, (D, KVD), jnp.float32, -4.6, -2.3)
    vals = unit * jnp.clip(jnp.exp(expo), 0.01, 0.1)
    return vals.astype(jnp.float32)


def cache_keys(key):
    base = jax.random.normal(key, (N_DP, N_FSDP, ROWS, CTX, HD), jnp.float32)
    base = jnp.clip(base, -5.0, 5.0)
    second = base[:, :, :, 1, :]
    return base.at[:, :, :, 1, :].set(second)


def draw_k_cache(key, part):
    keys = cache_keys(key)
    return keys.astype(jnp.bfloat16)


def draw_queries(key, part):
    strength = 0.0
    cached = cache_keys(key)
    key = jax.random.fold_in(key, 23)
    vals = jax.random.normal(key, (STEPS, N_DP, N_FSDP, ROWS, GQ * HD), jnp.float32)
    vals = jnp.clip(vals, -6.0, 6.0)
    first = cached[:, :, :, 0, :]
    rowid = jnp.arange(ROWS)[:, None]
    stepid = jnp.arange(STEPS)[:, None, None, None, None]
    strong = 9.0 * (1.0 + ((rowid + stepid) % 3).astype(jnp.float32))
    aligned = strong * first[None]
    chosen = (jnp.arange(ROWS) < 2)[:, None] * (strength > 0.5)
    head0 = jnp.where(chosen, aligned, vals[..., :HD])
    vals = vals.at[..., :HD].set(head0)
    return vals.astype(jnp.bfloat16)


def draw_cache_len(key, part):
    key = jax.random.fold_in(key, 37)
    lens = jax.random.randint(key, (N_DP, REPL, ROWS), CTX // 8, CTX - STEPS + 1)
    return lens.at[:, :, 0].set(CTX - STEPS).astype(jnp.int32)


def block_scale(rng, dims, cuts, least, top_value):
    def one(axis_at, parts):
        draws = jax.random.uniform(jax.random.fold_in(jax.random.fold_in(rng, 6), axis_at), (parts,), jnp.float32, least / len(cuts), top_value / len(cuts))
        return jnp.repeat(jnp.exp(draws), dims[axis_at] // parts).reshape((-1,) + (1,) * (len(dims) - axis_at - 1))

    loudness = one(*cuts[0])
    for cut in cuts[1:]:
        loudness = loudness * one(*cut)
    return loudness


def bell_draw(stream_key, shape, scale, most, shards=(), kind=jnp.bfloat16):
    factor_of = block_scale(stream_key, shape, shards, -0.22, 0.18) if shards else 1.0
    entries = jax.random.normal(stream_key, shape, jnp.float32) * scale * factor_of
    return jnp.minimum(jnp.maximum(entries, -most), most).astype(kind)


def setup_inputs(seed: int = 0) -> dict:
    key_of = jax.random.split(jax.random.key(seed), 12)
    return {
        "acts": draw_acts(jax.random.fold_in(key_of[11], 71), 0),
        "cotangent": bell_draw(key_of[1], (TOKENS, KVD), 1.0, 6.0, ((0, 128),)),
        "master": draw_master(jax.random.fold_in(key_of[11], 71), 0),
        "moment1": draw_moment1(jax.random.fold_in(key_of[11], 71), 0),
        "moment2": draw_moment2(jax.random.fold_in(key_of[11], 71), 0),
        "hidden_in": bell_draw(key_of[5], (STEPS, N_DP, N_FSDP, ROWS, D // KVH), 1.0, 6.0, ((1, 4), (2, 32))),
        "k_cache": draw_k_cache(jax.random.fold_in(key_of[11], 71), 0),
        "v_cache": bell_draw(key_of[7], (N_DP, N_FSDP, ROWS, CTX, HD), 1.0, 6.0, ((0, 4), (1, 32))),
        "k_new": bell_draw(key_of[8], (STEPS, N_DP, N_FSDP, ROWS, HD), 2.5, 15.0, ((1, 4), (2, 32))),
        "queries": draw_queries(jax.random.fold_in(key_of[11], 71), 0),
        "cache_len": draw_cache_len(jax.random.fold_in(key_of[11], 71), 0),
    }


def attend(query, keys, values, knew, vnew, lens):
    steps, rows = (query.shape[0], query.shape[1])
    hsize = keys.shape[-1]
    qh = query.reshape(steps, rows, -1, hsize).astype(jnp.float32)
    scale = hsize ** (-0.5)
    sc = jnp.einsum('srhd,rcd->srhc', qh, keys.astype(jnp.float32)) * scale
    sn = jnp.einsum('srhd,trd->srht', qh, knew.astype(jnp.float32)) * scale
    cmask = jnp.arange(keys.shape[1])[None, :] < lens[:, None]
    nmask = jnp.arange(steps)[None, :] <= jnp.arange(steps)[:, None]
    sc = jnp.where(cmask[None, :, None, :], sc, -1e+30)
    sn = jnp.where(nmask[:, None, None, :], sn, -1e+30)
    top = jnp.maximum(lax.optimization_barrier(jnp.max(sc, -1)), lax.optimization_barrier(jnp.max(sn, -1)))
    ec = jnp.exp(sc - top[..., None])
    en = jnp.exp(sn - top[..., None])
    den = lax.optimization_barrier(jnp.sum(ec, -1)) + lax.optimization_barrier(jnp.sum(en, -1))
    pc = ec.astype(jnp.bfloat16).astype(jnp.float32)
    pn = en.astype(jnp.bfloat16).astype(jnp.float32)
    out = jnp.einsum('srhc,rcd->srhd', pc, values.astype(jnp.float32))
    out = out + jnp.einsum('srht,trd->srhd', pn, vnew.astype(jnp.float32))
    return (out / den[..., None]).reshape(steps, rows, -1).astype(jnp.bfloat16)

def reference(acts, cotangent, master, moment1, moment2, hidden_in, k_cache, v_cache, k_new, queries, cache_len):
    grad = lax.dot_general(acts, cotangent, (((0,), (0,)), ((), ())), preferred_element_type=jnp.float32)
    gnorm = jnp.sqrt(jnp.sum(grad * grad))
    clipped = grad * jnp.minimum(1.0, 1.0 / (gnorm + 1e-06))
    mom = 0.9 * moment1 + 0.1 * clipped
    sec = 0.95 * moment2 + 0.05 * clipped * clipped
    update = mom / (1.0 - 0.9 ** 10) / (jnp.sqrt(sec / (1.0 - 0.95 ** 10)) + 1e-08)
    new_master = master - 0.1 * (update + 0.1 * master)
    w_roll = new_master.astype(jnp.bfloat16)
    ndp, nfs = (hidden_in.shape[1], hidden_in.shape[2])
    feats = hidden_in.reshape(STEPS, ndp, REPL, KVH, ROWS, D // KVH)
    feats = feats.transpose(0, 1, 2, 4, 3, 5).reshape(-1, D)
    vall = jnp.dot(feats, w_roll, preferred_element_type=jnp.float32) * (32.0 * D ** (-0.5))
    vall = vall.astype(jnp.bfloat16).reshape(STEPS, ndp, REPL, ROWS, KVH, HD)
    vnew = vall.transpose(0, 1, 2, 4, 3, 5).reshape(STEPS, ndp * nfs, ROWS, HD)
    lens = jnp.repeat(cache_len, KVH, axis=1).reshape(ndp * nfs, ROWS)
    qall = queries.reshape(STEPS, ndp * nfs, ROWS, -1).transpose(1, 0, 2, 3)
    kall = k_new.reshape(STEPS, ndp * nfs, ROWS, HD).transpose(1, 0, 2, 3)
    vnall = vnew.transpose(1, 0, 2, 3)
    kc = k_cache.reshape(ndp * nfs, ROWS, CTX, HD)
    vc = v_cache.reshape(ndp * nfs, ROWS, CTX, HD)

    def one(items):
        return attend(items[0], items[1], items[2], items[3], items[4], items[5])
    outs = lax.map(one, (qall, kc, vc, kall, vnall, lens))
    attn_out = outs.transpose(1, 0, 2, 3).reshape(STEPS, ndp, nfs, ROWS, -1)
    return (new_master, attn_out)
```

```python
import functools

import jax
import jax.numpy as jnp
from jax import lax
from jax.experimental import pallas as pl
from jax.experimental.pallas import tpu as pltpu
from jax.sharding import PartitionSpec as P

MESH = pl.DeviceIdType.MESH
F32 = jnp.float32
BF16 = jnp.bfloat16
PARTS = ((0, 176), (176, 176), (352, 160))
NT = (((1,), (1,)), ((), ()))


def coordinates():
    f, d = lax.axis_index("fsdp"), lax.axis_index("dp")
    return ((f // 4) % 4, f % 4, (d // 2) * 2 + f // 16), d % 2


def device(pos, core):
    x, y, z = pos
    return ((z % 2) * 16 + x * 4 + y, (z // 2) * 2 + core)


def shifted(pos, dim, delta):
    return tuple((v + delta) % 4 if i == dim else v for i, v in enumerate(pos))


def kernel(
    lens, acts, cot, master, mom1, mom2, hid, keys, vals, knew, query,
    nm_out, at_out,
    abuf, cbuf, ct, g0, g1, g2, ra0, ra1, ra2, s0, s1, s2, rb0, rb1, rb2, t0, t1, t2, rc0, rc1, rc2,
    ms, gt, nsend, nrecv, nmx, nmr, wsend, wbuf, vf, vs, vr,
    kbuf, vbuf, qbuf, knbuf, hbuf, qs, kns, acc, ens, accn, enn,
    loc, asend, arecv, xsend, xrecv, p1s, p1r, p2s, p2r, p3s, p3r, nss, nsr, ws, wr, fs, fr, vss, vsr, osend, orecv,
):
    pos, core = coordinates()
    x, y, z = pos
    other = 1 - core
    me = device(pos, core)
    sib = device(pos, other)
    gs, ras, ss, rbs, ts, rcs = (g0, g1, g2), (ra0, ra1, ra2), (s0, s1, s2), (rb0, rb1, rb2), (t0, t1, t2), (rc0, rc1, rc2)

    def copy(src, dst, sem):
        return pltpu.make_async_copy(src, dst, sem)

    def remote(src, dst, ssem, rsem, dev):
        return pltpu.make_async_remote_copy(
            src_ref=src, dst_ref=dst, send_sem=ssem, recv_sem=rsem, device_id=dev, device_id_type=MESH
        )

    def drain(ref, sem):
        pltpu.make_async_copy(ref, ref, sem).wait()

    def lanes(k, j):
        xb, yb = j // 4, j % 4
        zb = (k + 8 - xb - yb) % 4
        return pl.ds(pl.multiple_of((((zb % 2) * 16 + xb * 4 + yb) * 2 + zb // 2) * 128, 128), 128)

    half = pl.ds(pl.multiple_of(core * 512, 512), 512)
    far = pl.ds(pl.multiple_of(other * 512, 512), 512)
    mine = pl.ds(pl.multiple_of(core * 64, 64), 64)
    theirs = pl.ds(pl.multiple_of(other * 64, 64), 64)

    barrier = pltpu.get_barrier_semaphore()
    pl.semaphore_signal(barrier, inc=1, device_id=sib, device_id_type=MESH)
    for dim in range(3):
        for delta in (1, 2, 3):
            pl.semaphore_signal(barrier, inc=1, device_id=device(shifted(pos, dim, delta), core), device_id_type=MESH)

    copy(cot.at[:, half], cbuf.at[0], loc.at[4]).start()
    for k in range(4):
        @pl.loop(0, 16)
        def _(j):
            to = pl.ds(pl.multiple_of(j * 128, 128), 128)
            copy(acts.at[:, lanes(k, j)], abuf.at[k, pl.ds(0, 512), to], loc.at[k]).start()
    copy(query, qbuf, loc.at[6]).start()
    copy(knew, knbuf, loc.at[7]).start()
    copy(keys, kbuf, loc.at[8]).start()
    copy(vals, vbuf, loc.at[9]).start()
    for i, ref in enumerate((master, mom1, mom2)):
        copy(ref.at[:, half], ms.at[i, mine], loc.at[10 + i]).start()
    copy(hid, hbuf, loc.at[5]).start()

    pl.semaphore_wait(barrier, 10)

    remote(cot.at[:, far], cbuf.at[1], xsend.at[0], xrecv.at[0], sib).start()
    for k in range(4):
        @pl.loop(0, 16)
        def _(j):
            to = pl.ds(pl.multiple_of(j * 128, 128), 128)
            remote(acts.at[:, lanes(k, j)], abuf.at[k, pl.ds(512, 512), to], asend.at[k], arecv.at[k], sib).start()
    for i, ref in enumerate((master, mom1, mom2)):
        remote(ref.at[:, far], ms.at[i, mine], xsend.at[1 + i], xrecv.at[1 + i], sib).start()

    copy(cot.at[:, half], cbuf.at[0], loc.at[4]).wait()
    ct[:, 0:512] = cbuf[0].T
    drain(cbuf.at[1], xrecv.at[0])
    ct[:, 512:1024] = cbuf[1].T

    for k in range(4):
        drain(abuf.at[k, pl.ds(0, 512)], loc.at[k])
        drain(abuf.at[k, pl.ds(512, 512)], arecv.at[k])

        @pl.loop(0, 8)
        def _(jp):
            cols = pl.ds(pl.multiple_of(jp * 256, 256), 256)
            res = jnp.dot(ct[...], abuf[k, :, cols], preferred_element_type=F32).astype(BF16)
            xb = jp // 2
            for e in range(2):
                yb = (jp % 2) * 2 + e
                zb = (k + 8 - xb - yb) % 4
                piece = res[:, e * 128 : (e + 1) * 128]
                g0[k, xb, yb] = piece[0:176]
                g1[k, yb, zb] = piece[176:352]
                g2[k, zb, xb] = piece[352:512]

        for p in range(3):
            for delta in (1, 2, 3):
                to = shifted(pos, p, delta)
                remote(
                    gs[p].at[k, to[p]], ras[p].at[k, delta - 1], p1s.at[p], p1r.at[k, p], device(to, core)
                ).start()

    copy(query, qbuf, loc.at[6]).wait()
    copy(knew, knbuf, loc.at[7]).wait()
    for s in range(4):
        for h in range(8):
            qs[pl.ds(s * 8 + h, 32, stride=32), :] = qbuf[s, :, h * 128 : (h + 1) * 128].astype(F32)
    kns[...] = jnp.zeros_like(kns)
    for s in range(4):
        kns[pl.ds(s, 32, stride=8), :] = knbuf[s].astype(F32)
    copy(keys, kbuf, loc.at[8]).wait()
    copy(vals, vbuf, loc.at[9]).wait()
    replica = (z % 2) * 2 + x // 2
    scale = 128 ** (-0.5)

    def attend(i):
        rows = pl.ds(pl.multiple_of(i * 32, 32), 32)
        qi = qs[rows, :].astype(BF16)
        sc = lax.dot_general(qi, kbuf[i], NT, preferred_element_type=F32) * scale
        slot = lax.broadcasted_iota(jnp.int32, (32, 512), 1)
        sc = jnp.where(slot < lens[replica, i], sc, -1e30)
        kn = kns[pl.ds(pl.multiple_of(i * 8, 8), 8), :].astype(BF16)
        sn = lax.dot_general(qi, kn, NT, preferred_element_type=F32) * scale
        step = lax.broadcasted_iota(jnp.int32, (32, 8), 0) // 8
        sn = jnp.where(lax.broadcasted_iota(jnp.int32, (32, 8), 1) <= step, sn, -1e30)
        top = jnp.maximum(jnp.max(sc, 1, keepdims=True), jnp.max(sn, 1, keepdims=True))
        ec = jnp.exp(sc - top)
        en = jnp.exp(sn - top)
        inv = 1.0 / (jnp.sum(ec, 1, keepdims=True) + jnp.sum(en, 1, keepdims=True))
        out = jnp.dot(ec.astype(BF16), vbuf[i], preferred_element_type=F32)
        acc[rows, :] = out * inv
        ens[rows, 0:8] = en.astype(BF16).astype(F32) * inv

    def attend_rows(first):
        @pl.loop(0, 4)
        def _(i):
            attend(first + 2 * i)
            attend(first + 2 * i + 1)

    def first_sum(k):
        for p in range(3):
            b = (p + 1) % 3
            drain(ras[p].at[k], p1r.at[k, p])

            @pl.loop(0, 4)
            def _(i):
                total = gs[p][k, pos[p], i].astype(F32)
                for slot in range(3):
                    total += ras[p][k, slot, i].astype(F32)
                ss[p][k, i] = total.astype(BF16)

            for delta in (1, 2, 3):
                to = shifted(pos, b, delta)
                remote(
                    ss[p].at[k, to[b]], rbs[p].at[k, delta - 1], p2s.at[p], p2r.at[k, p], device(to, core)
                ).start()

    def second_sum(k):
        for p in range(3):
            b, c = (p + 1) % 3, (p + 2) % 3
            drain(rbs[p].at[k], p2r.at[k, p])
            total = ss[p][k, pos[b]].astype(F32)
            for slot in range(3):
                total += rbs[p][k, slot].astype(F32)
            ts[p][k] = total.astype(BF16)
            target = (k + 8 - pos[p] - pos[b]) % 4
            delta = (target + 4 - pos[c]) % 4

            @pl.when(delta != 0)
            def _():
                remote(
                    ts[p].at[k], rcs[p].at[delta - 1], p3s.at[p], p3r.at[p], device(shifted(pos, c, delta), core)
                ).start()

    attend_rows(0)
    first_sum(0)
    attend_rows(8)
    first_sum(1)
    second_sum(0)
    attend_rows(16)
    first_sum(2)
    second_sum(1)
    attend_rows(24)
    for j in range(32):
        accn[j] = acc[pl.ds(j, 32, stride=32), :]
        enn[j] = ens[pl.ds(j, 32, stride=32), :]
    first_sum(3)
    second_sum(2)
    second_sum(3)

    own = (x + y + z) % 4
    for p, (first, size) in enumerate(PARTS):
        drain(rcs[p], p3r.at[p])
        total = ts[p][own].astype(F32)
        for slot in range(3):
            total += rcs[p][slot].astype(F32)
        gt[pl.ds(first, size), :] = total

    square = jnp.zeros((8, 128), F32)
    for i in range(64):
        part = gt[pl.ds(i * 8, 8), :]
        square += part * part
    for stage in range(4):
        nsend[stage] = square
        if stage == 0:
            remote(nsend.at[0], nrecv.at[0, 0], nss.at[0], nsr.at[0], sib).start()
            drain(nrecv.at[0, 0], nsr.at[0])
            square += nrecv[0, 0]
        else:
            for delta in (1, 2, 3):
                remote(
                    nsend.at[stage], nrecv.at[stage, delta - 1], nss.at[stage], nsr.at[stage],
                    device(shifted(pos, stage - 1, delta), core),
                ).start()
            drain(nrecv.at[stage], nsr.at[stage])
            for slot in range(3):
                square += nrecv[stage, slot]
    gnorm = jnp.sqrt(jnp.sum(square, keepdims=True))
    clip = jnp.minimum(1.0, 1.0 / (gnorm + 1e-06))

    for i in range(3):
        drain(ms.at[i, mine], loc.at[10 + i])
        drain(ms.at[i, theirs], xrecv.at[1 + i])
    for j in range(4):
        cols = slice(j * 128, (j + 1) * 128)
        clipped = gt[pl.ds(j * 128, 128), :].T * clip
        mom = 0.9 * ms[1, :, cols] + 0.1 * clipped
        sec = 0.95 * ms[2, :, cols] + 0.05 * clipped * clipped
        update = mom / (1.0 - 0.9**10) / (jnp.sqrt(sec / (1.0 - 0.95**10)) + 1e-08)
        weights = ms[0, :, cols]
        weights = weights - 0.1 * (update + 0.1 * weights)
        nmx[:, cols] = weights
        wsend[:, cols] = weights.astype(BF16)

    place = pl.ds(pl.multiple_of((y * 2 + z // 2) * 128, 128), 128)
    number = (y % 2) * 4 + (z // 2) * 2 + core
    to_core = y // 2

    def target(q):
        to = ((z % 2) + 2 * (q // 4), x, (z + q) % 4)
        same = (to[0] == x) & (to[1] == y) & (to[2] == z) & (to_core == core)
        return device(to, to_core), same

    @pl.loop(0, 8)
    def _(q):
        dev, same = target(q)

        @pl.when(jnp.logical_not(same))
        def _():
            remote(wsend, wbuf.at[place, half], ws.at[q], wr.at[number], dev).start()

        @pl.when(same)
        def _():
            copy(wsend, wbuf.at[place, half], wr.at[number]).start()

    remote(nmx.at[theirs], nmr, osend.at[0], orecv.at[0], sib).start()
    nm_out[:, half] = nmx[mine, :]
    copy(hid, hbuf, loc.at[5]).wait()

    @pl.loop(0, 8)
    def _(sl):
        rows = pl.ds(pl.multiple_of(((2 * core + sl // 4) * 2 + (sl // 2) % 2) * 128, 128), 128)
        cols = pl.ds(pl.multiple_of((sl % 2) * 512, 512), 512)
        drain(wbuf.at[rows, cols], wr.at[sl])
        remote(wbuf.at[rows, cols], wbuf.at[rows, cols], fs.at[0], fr.at[0], sib).start()

    @pl.loop(0, 4)
    def _(n):
        cols = pl.ds(pl.multiple_of(n * 256, 256), 256)
        res = jnp.dot(hbuf[:, half], wbuf[half, cols], preferred_element_type=F32)
        vf[2 * n] = res[:, 0:128]
        vf[2 * n + 1] = res[:, 128:256]

    drain(nmr, orecv.at[0])
    nm_out[:, far] = nmr[...]
    drain(wbuf.at[far], fr.at[0])
    head = (x % 2) * 4 + y

    @pl.loop(0, 4)
    def _(n):
        cols = pl.ds(pl.multiple_of(n * 256, 256), 256)
        res = jnp.dot(hbuf[:, far], wbuf[far, cols], preferred_element_type=F32)
        for e in range(2):
            to_head = 2 * n + e
            total = vf[to_head] + res[:, e * 128 : (e + 1) * 128]
            vf[to_head] = total
            vs[to_head] = total.astype(BF16)
            delta = (to_head + 8 - head) % 8
            to = ((x // 2) * 2 + to_head // 4, to_head % 4, z)

            @pl.when(delta != 0)
            def _():
                remote(vs.at[to_head], vr.at[delta - 1], vss.at[0], vsr.at[0], device(to, core)).start()

    drain(vr, vsr.at[0])
    total = vf[head]
    for slot in range(7):
        total += vr[slot].astype(F32)
    vnew = (total * (32.0 * 8192 ** (-0.5))).astype(BF16).astype(F32)
    for s in range(4):
        for h in range(8):
            out = accn[s * 8 + h]
            weight = enn[s * 8 + h]
            for t in range(s + 1):
                out += weight[:, t : t + 1] * vnew[t * 32 : (t + 1) * 32]
            at_out[s, :, h * 128 : (h + 1) * 128] = out.astype(BF16)

    drain(cbuf.at[1], xsend.at[0])
    for i in range(3):
        drain(ms.at[i, theirs], xsend.at[1 + i])
    for k in range(4):
        drain(abuf.at[k, pl.ds(512, 512)], asend.at[k])
    for p in range(3):
        drain(ras[p], p1s.at[p])
        drain(rbs[p], p2s.at[p])
        drain(rcs[p], p3s.at[p])
    drain(nrecv.at[0, 0], nss.at[0])
    for stage in range(1, 4):
        drain(nrecv.at[stage], nss.at[stage])

    @pl.loop(0, 8)
    def _(q):
        _, same = target(q)

        @pl.when(jnp.logical_not(same))
        def _():
            drain(wsend, ws.at[q])

    drain(nmr, osend.at[0])
    drain(wbuf.at[half], fs.at[0])
    drain(vr, vss.at[0])


def scratch():
    v, sem = pltpu.VMEM, pltpu.SemaphoreType.DMA
    sizes = [size for _, size in PARTS]
    return [
        v((4, 1024, 2048), BF16), v((2, 512, 512), BF16), v((512, 1024), BF16),
        *[v((4, 4, 4, n, 128), BF16) for n in sizes],
        *[v((4, 3, 4, n, 128), BF16) for n in sizes],
        *[v((4, 4, n, 128), BF16) for n in sizes],
        *[v((4, 3, n, 128), BF16) for n in sizes],
        *[v((4, n, 128), BF16) for n in sizes],
        *[v((3, n, 128), BF16) for n in sizes],
        v((3, 128, 512), F32), v((512, 128), F32), v((4, 8, 128), F32), v((4, 3, 8, 128), F32),
        v((128, 512), F32), v((64, 512), F32), v((128, 512), BF16), v((1024, 1024), BF16),
        v((8, 128, 128), F32), v((8, 128, 128), BF16), v((7, 128, 128), BF16),
        v((32, 512, 128), BF16), v((32, 512, 128), BF16), v((4, 32, 1024), BF16), v((4, 32, 128), BF16), v((128, 1024), BF16),
        v((1024, 128), F32), v((256, 128), F32), v((1024, 128), F32), v((1024, 128), F32), v((32, 32, 128), F32), v((32, 32, 128), F32),
        sem((13,)), sem((4,)), sem((4,)), sem((4,)), sem((4,)),
        sem((3,)), sem((4, 3)), sem((3,)), sem((4, 3)), sem((3,)), sem((3,)),
        sem((4,)), sem((4,)), sem((8,)), sem((8,)), sem((1,)), sem((1,)), sem((1,)), sem((1,)), sem((1,)), sem((1,)),
    ]


def on_device(
    acts, cotangent, master, moment1, moment2, hidden_in, k_cache, v_cache, k_new, queries, cache_len
):
    place = pl.BlockSpec(memory_space=pl.ANY)
    new_master, out = pl.pallas_call(
        kernel,
        name="update_and_decode",
        out_shape=(jax.ShapeDtypeStruct((64, 1024), F32), jax.ShapeDtypeStruct((4, 32, 1024), BF16)),
        in_specs=[pl.BlockSpec(memory_space=pltpu.SMEM)] + [place] * 10,
        out_specs=(pl.BlockSpec(memory_space=pltpu.VMEM), pl.BlockSpec(memory_space=pltpu.VMEM)),
        scratch_shapes=scratch(),
        compiler_params=pltpu.CompilerParams(
            collective_id=0, has_side_effects=True, vmem_limit_bytes=60 * 2**20
        ),
    )(
        cache_len[0], acts, cotangent, master, moment1, moment2, hidden_in.reshape(128, 1024),
        k_cache[0, 0], v_cache[0, 0], k_new[:, 0, 0], queries[:, 0, 0],
    )
    return new_master, out.reshape(4, 1, 1, 32, 1024)


def solution(mesh):
    rows = P(("fsdp", "dp"), None)
    in_specs = (
        rows, rows, rows, rows, rows,
        P(None, "dp", "fsdp", None, None),
        P("dp", "fsdp", None, None, None),
        P("dp", "fsdp", None, None, None),
        P(None, "dp", "fsdp", None, None),
        P(None, "dp", "fsdp", None, None),
        P("dp", None, None),
    )
    out_specs = (rows, P(None, "dp", "fsdp", None, None))
    return jax.shard_map(on_device, mesh=mesh, in_specs=in_specs, out_specs=out_specs, check_vma=False)
```

```python
import functools

import jax
import jax.numpy as jnp
from jax import lax
from jax.experimental import pallas as pl
from jax.experimental.pallas import tpu as pltpu
from jax.sharding import PartitionSpec as P

MESH = pl.DeviceIdType.MESH
F32 = jnp.float32
BF16 = jnp.bfloat16
PARTS = ((0, 176), (176, 176), (352, 160))
NT = (((1,), (1,)), ((), ()))


def coordinates():
    f, d = lax.axis_index("fsdp"), lax.axis_index("dp")
    return ((f // 4) % 4, f % 4, (d // 2) * 2 + f // 16), d % 2


def device(pos, core):
    x, y, z = pos
    return ((z % 2) * 16 + x * 4 + y, (z // 2) * 2 + core)


def shifted(pos, dim, delta):
    return tuple((v + delta) % 4 if i == dim else v for i, v in enumerate(pos))


def kernel(
    lens, acts, cot, master, mom1, mom2, hid, keys, vals, knew, query,
    nm_out, at_out,
    abuf, cbuf, ct, g0, g1, g2, ra0, ra1, ra2, rb0, rb1, rb2, s0, s1, s2, rc0, rc1, rc2, t0, t1, t2, rd0, rd1, rd2,
    ms, gt, nsend, nra, nrb, nmx, nmr, wsend, wbuf, vs, vr,
    kbuf, vbuf, qbuf, knbuf, hbuf, qs, kns, acc, ens, accn, enn,
    loc, asend, arecv, xsend, xrecv, pas, par, pbs, pbr, p2s, p2r, p3s, p3r, nss, nsr, ws, wr, hs, hr, hfs, hfr, vss, vsr, osend, orecv,
):
    pos, core = coordinates()
    x, y, z = pos
    other = 1 - core
    me = device(pos, core)
    sib = device(pos, other)
    gs, ras, rbs, ss, rcs, ts, rds = (
        (g0, g1, g2), (ra0, ra1, ra2), (rb0, rb1, rb2), (s0, s1, s2), (rc0, rc1, rc2), (t0, t1, t2), (rd0, rd1, rd2)
    )

    def copy(src, dst, sem):
        return pltpu.make_async_copy(src, dst, sem)

    def remote(src, dst, ssem, rsem, dev):
        return pltpu.make_async_remote_copy(
            src_ref=src, dst_ref=dst, send_sem=ssem, recv_sem=rsem, device_id=dev, device_id_type=MESH
        )

    def drain(ref, sem):
        pltpu.make_async_copy(ref, ref, sem).wait()

    def lanes(k, j):
        xb, yb = j // 4, j % 4
        zb = (k + 8 - xb - yb) % 4
        return pl.ds(pl.multiple_of((((zb % 2) * 16 + xb * 4 + yb) * 2 + zb // 2) * 128, 128), 128)

    half = pl.ds(pl.multiple_of(core * 512, 512), 512)
    far = pl.ds(pl.multiple_of(other * 512, 512), 512)
    mine = pl.ds(pl.multiple_of(core * 64, 64), 64)
    theirs = pl.ds(pl.multiple_of(other * 64, 64), 64)

    pair = x // 2
    rows_here = pl.ds(pl.multiple_of(core * 128, 128), 128)
    rows_there = pl.ds(pl.multiple_of(other * 128, 128), 128)

    def mirror(p):
        same = x // 2 == p
        return jnp.where(same, x, 3 - x), jnp.where(same, 0, 1)

    def hidden_target(yb):
        to = (jnp.where(y // 2 == pair, y, 3 - y), yb, z)
        group = jnp.where(y // 2 == pair, 0, 2) + x % 2
        src = hid.at[:, pl.ds(pl.multiple_of(yb * 256, 256), 256)]
        dst = hbuf.at[rows_here, pl.ds(pl.multiple_of(group * 256, 256), 256)]
        return to, src, dst, (to[0] == x) & (yb == y)

    barrier = pltpu.get_barrier_semaphore()
    pl.semaphore_signal(barrier, inc=1, device_id=sib, device_id_type=MESH)
    for dim in range(3):
        for delta in (1, 2, 3):
            pl.semaphore_signal(barrier, inc=1, device_id=device(shifted(pos, dim, delta), core), device_id_type=MESH)
    for delta in (1, 2, 3):
        to = (pair * 2 + 1 - x % 2, (y + delta) % 4, z)
        pl.semaphore_signal(barrier, inc=1, device_id=device(to, core), device_id_type=MESH)

    copy(cot.at[:, half], cbuf.at[0], loc.at[4]).start()
    for k in range(4):
        @pl.loop(0, 16)
        def _(j):
            to = pl.ds(pl.multiple_of(j * 128, 128), 128)
            copy(acts.at[:, lanes(k, j)], abuf.at[k, pl.ds(0, 512), to], loc.at[k]).start()
    copy(query, qbuf, loc.at[6]).start()
    copy(knew, knbuf, loc.at[7]).start()
    copy(keys, kbuf, loc.at[8]).start()
    copy(vals, vbuf, loc.at[9]).start()
    for i, ref in enumerate((master, mom1, mom2)):
        copy(ref.at[:, half], ms.at[i, mine], loc.at[10 + i]).start()

    pl.semaphore_wait(barrier, 13)

    remote(cot.at[:, far], cbuf.at[1], xsend.at[0], xrecv.at[0], sib).start()
    for k in range(4):
        @pl.loop(0, 16)
        def _(j):
            to = pl.ds(pl.multiple_of(j * 128, 128), 128)
            remote(acts.at[:, lanes(k, j)], abuf.at[k, pl.ds(512, 512), to], asend.at[k], arecv.at[k], sib).start()

    @pl.loop(0, 4)
    def _(yb):
        to, src, dst, same = hidden_target(yb)

        @pl.when(jnp.logical_not(same))
        def _():
            remote(src, dst, hs.at[yb], hr.at[0], device(to, core)).start()

        @pl.when(same)
        def _():
            copy(src, dst, hr.at[0]).start()

    for i, ref in enumerate((master, mom1, mom2)):
        remote(ref.at[:, far], ms.at[i, mine], xsend.at[1 + i], xrecv.at[1 + i], sib).start()

    copy(cot.at[:, half], cbuf.at[0], loc.at[4]).wait()
    ct[:, 0:512] = cbuf[0].T
    drain(cbuf.at[1], xrecv.at[0])
    ct[:, 512:1024] = cbuf[1].T

    def pass_on(k):
        for p in range(3):
            g, ra, rb = gs[p], ras[p], rbs[p]
            up, down = shifted(pos, p, 1), shifted(pos, p, 3)
            drain(ra.at[k], par.at[k, p])

            @pl.loop(0, 2)
            def _(i):
                g[k, up[p], i] = (g[k, up[p], i].astype(F32) + ra[k, 0, i].astype(F32)).astype(BF16)
                g[k, down[p], 2 + i] = (g[k, down[p], 2 + i].astype(F32) + ra[k, 1, i].astype(F32)).astype(BF16)

            remote(g.at[k, up[p], 0:2], rb.at[k, 0, 0:2], pbs.at[p], pbr.at[k, p], device(up, core)).start()
            remote(g.at[k, down[p], 2:4], rb.at[k, 1, 2:4], pbs.at[p], pbr.at[k, p], device(down, core)).start()

    for k in range(4):
        drain(abuf.at[k, pl.ds(0, 512)], loc.at[k])
        drain(abuf.at[k, pl.ds(512, 512)], arecv.at[k])

        @pl.loop(0, 4)
        def _(xb):
            cols = pl.ds(pl.multiple_of(xb * 512, 512), 512)
            res = jnp.dot(ct[...], abuf[k, :, cols], preferred_element_type=F32).astype(BF16)
            for yb in range(4):
                zb = (k + 8 - xb - yb) % 4
                piece = res[:, yb * 128 : (yb + 1) * 128]
                g0[k, xb, yb] = piece[0:176]
                g1[k, yb, zb] = piece[176:352]
                g2[k, zb, xb] = piece[352:512]

        for p in range(3):
            g, ra, rb = gs[p], ras[p], rbs[p]
            up, down, opposite = shifted(pos, p, 1), shifted(pos, p, 3), (pos[p] + 2) % 4
            to_up, to_down = device(up, core), device(down, core)
            remote(g.at[k, opposite, 0:2], ra.at[k, 0], pas.at[p], par.at[k, p], to_up).start()
            remote(g.at[k, opposite, 2:4], ra.at[k, 1], pas.at[p], par.at[k, p], to_down).start()
            remote(g.at[k, up[p], 2:4], rb.at[k, 0, 2:4], pbs.at[p], pbr.at[k, p], to_up).start()
            remote(g.at[k, down[p], 0:2], rb.at[k, 1, 0:2], pbs.at[p], pbr.at[k, p], to_down).start()
        if k > 0:
            pass_on(k - 1)

    drain(hbuf.at[rows_here], hr.at[0])
    remote(hbuf.at[rows_here], hbuf.at[rows_here], hfs.at[0], hfr.at[0], sib).start()

    copy(query, qbuf, loc.at[6]).wait()
    copy(knew, knbuf, loc.at[7]).wait()
    for s in range(4):
        for h in range(8):
            qs[pl.ds(s * 8 + h, 32, stride=32), :] = qbuf[s, :, h * 128 : (h + 1) * 128].astype(F32)
    kns[...] = jnp.zeros_like(kns)
    for s in range(4):
        kns[pl.ds(s, 32, stride=8), :] = knbuf[s].astype(F32)
    copy(keys, kbuf, loc.at[8]).wait()
    copy(vals, vbuf, loc.at[9]).wait()
    replica = (z % 2) * 2 + x // 2
    scale = 128 ** (-0.5)

    def attend(i):
        rows = pl.ds(pl.multiple_of(i * 32, 32), 32)
        qi = qs[rows, :].astype(BF16)
        sc = lax.dot_general(qi, kbuf[i], NT, preferred_element_type=F32) * scale
        slot = lax.broadcasted_iota(jnp.int32, (32, 512), 1)
        sc = jnp.where(slot < lens[replica, i], sc, -1e30)
        kn = kns[pl.ds(pl.multiple_of(i * 8, 8), 8), :].astype(BF16)
        sn = lax.dot_general(qi, kn, NT, preferred_element_type=F32) * scale
        step = lax.broadcasted_iota(jnp.int32, (32, 8), 0) // 8
        sn = jnp.where(lax.broadcasted_iota(jnp.int32, (32, 8), 1) <= step, sn, -1e30)
        top = jnp.maximum(jnp.max(sc, 1, keepdims=True), jnp.max(sn, 1, keepdims=True))
        ec = jnp.exp(sc - top)
        en = jnp.exp(sn - top)
        inv = 1.0 / (jnp.sum(ec, 1, keepdims=True) + jnp.sum(en, 1, keepdims=True))
        out = jnp.dot(ec.astype(BF16), vbuf[i], preferred_element_type=F32)
        acc[rows, :] = out * inv
        ens[rows, 0:8] = en.astype(BF16).astype(F32) * inv

    def attend_rows(first):
        @pl.loop(0, 4)
        def _(i):
            attend(first + 2 * i)
            attend(first + 2 * i + 1)

    def first_sum(k):
        for p in range(3):
            b = (p + 1) % 3
            drain(rbs[p].at[k], pbr.at[k, p])

            @pl.loop(0, 4)
            def _(i):
                total = gs[p][k, pos[p], i].astype(F32) + rbs[p][k, 0, i].astype(F32) + rbs[p][k, 1, i].astype(F32)
                ss[p][k, i] = total.astype(BF16)

            for delta in (1, 2, 3):
                to = shifted(pos, b, delta)
                remote(
                    ss[p].at[k, to[b]], rcs[p].at[k, delta - 1], p2s.at[p], p2r.at[k, p], device(to, core)
                ).start()

    def second_sum(k):
        for p in range(3):
            b, c = (p + 1) % 3, (p + 2) % 3
            drain(rcs[p].at[k], p2r.at[k, p])
            total = ss[p][k, pos[b]].astype(F32)
            for slot in range(3):
                total += rcs[p][k, slot].astype(F32)
            ts[p][k] = total.astype(BF16)
            target = (k + 8 - pos[p] - pos[b]) % 4
            delta = (target + 4 - pos[c]) % 4

            @pl.when(delta != 0)
            def _():
                remote(
                    ts[p].at[k], rds[p].at[delta - 1], p3s.at[p], p3r.at[p], device(shifted(pos, c, delta), core)
                ).start()

    attend_rows(0)
    pass_on(3)
    first_sum(0)
    attend_rows(8)
    first_sum(1)
    second_sum(0)
    attend_rows(16)
    first_sum(2)
    second_sum(1)
    attend_rows(24)
    for j in range(32):
        accn[j] = acc[pl.ds(j, 32, stride=32), :]
        enn[j] = ens[pl.ds(j, 32, stride=32), :]
    first_sum(3)
    second_sum(2)
    second_sum(3)

    own = (x + y + z) % 4
    for p, (first, size) in enumerate(PARTS):
        drain(rds[p], p3r.at[p])
        total = ts[p][own].astype(F32)
        for slot in range(3):
            total += rds[p][slot].astype(F32)
        gt[pl.ds(first, size), :] = total

    square = jnp.zeros((8, 128), F32)
    for i in range(64):
        part = gt[pl.ds(i * 8, 8), :]
        square += part * part
    nsend[0] = square
    for q in range(1, 8):
        to = device(((x + q // 2) % 4, y, z), (core + q) % 2)
        remote(nsend.at[0], nra.at[q - 1], nss.at[0], nsr.at[0], to).start()
    drain(nra, nsr.at[0])
    for slot in range(7):
        square += nra[slot]
    nsend[1] = square
    for q in range(1, 16):
        to = device((x, (y + q // 4) % 4, (z + q) % 4), core)
        remote(nsend.at[1], nrb.at[q - 1], nss.at[1], nsr.at[1], to).start()
    drain(nrb, nsr.at[1])
    for slot in range(15):
        square += nrb[slot]
    gnorm = jnp.sqrt(jnp.sum(square, keepdims=True))
    clip = jnp.minimum(1.0, 1.0 / (gnorm + 1e-06))

    for i in range(3):
        drain(ms.at[i, mine], loc.at[10 + i])
        drain(ms.at[i, theirs], xrecv.at[1 + i])
    for j in range(4):
        cols = slice(j * 128, (j + 1) * 128)
        clipped = gt[pl.ds(j * 128, 128), :].T * clip
        mom = 0.9 * ms[1, :, cols] + 0.1 * clipped
        sec = 0.95 * ms[2, :, cols] + 0.05 * clipped * clipped
        update = mom / (1.0 - 0.9**10) / (jnp.sqrt(sec / (1.0 - 0.95**10)) + 1e-08)
        weights = ms[0, :, cols]
        weights = weights - 0.1 * (update + 0.1 * weights)
        nmx[:, cols] = weights
        wsend[:, cols] = weights.astype(BF16)

    def weight_target(q):
        xb, far_pair = mirror(q // 4)
        zb = (z + q) % 4
        slot = far_pair * 4 + (z % 2) * 2 + z // 2
        dst = wbuf.at[pl.ds(pl.multiple_of(slot * 128, 128), 128), :]
        return (xb, y, zb), dst, (xb == x) & (zb == z)

    @pl.loop(0, 8)
    def _(q):
        to, dst, same = weight_target(q)

        @pl.when(jnp.logical_not(same))
        def _():
            remote(wsend, dst, ws.at[q], wr.at[0], device(to, core)).start()

        @pl.when(same)
        def _():
            copy(wsend, dst, wr.at[0]).start()

    remote(nmx.at[theirs], nmr, osend.at[0], orecv.at[0], sib).start()
    nm_out[:, half] = nmx[mine, :]
    drain(hbuf.at[rows_there], hfr.at[0])
    drain(nmr, orecv.at[0])
    nm_out[:, far] = nmr[...]
    drain(wbuf, wr.at[0])

    number = (x % 2) * 4 + y

    def value_target(q):
        to = (pair * 2 + core, q // 2, z)
        to_core = q % 2
        return to, to_core, (to[0] == x) & (to[1] == y) & (to_core == core)

    for n in range(2):
        res = jnp.dot(hbuf[...], wbuf[:, n * 256 : (n + 1) * 256], preferred_element_type=F32).astype(BF16)
        for e in range(2):
            for c in range(2):
                q = (n * 2 + e) * 2 + c
                vs[q] = res[c * 128 : (c + 1) * 128, e * 128 : (e + 1) * 128]
                to, to_core, same = value_target(q)

                @pl.when(jnp.logical_not(same))
                def _():
                    remote(vs.at[q], vr.at[number], vss.at[q], vsr.at[0], device(to, to_core)).start()

                @pl.when(same)
                def _():
                    copy(vs.at[q], vr.at[number], vsr.at[0]).start()

    drain(vr, vsr.at[0])
    total = vr[0].astype(F32)
    for slot in range(1, 8):
        total += vr[slot].astype(F32)
    vnew = (total * (32.0 * 8192 ** (-0.5))).astype(BF16).astype(F32)
    for s in range(4):
        for h in range(8):
            out = accn[s * 8 + h]
            weight = enn[s * 8 + h]
            for t in range(s + 1):
                out += weight[:, t : t + 1] * vnew[t * 32 : (t + 1) * 32]
            at_out[s, :, h * 128 : (h + 1) * 128] = out.astype(BF16)

    drain(cbuf.at[1], xsend.at[0])
    for i in range(3):
        drain(ms.at[i, theirs], xsend.at[1 + i])
    for k in range(4):
        drain(abuf.at[k, pl.ds(512, 512)], asend.at[k])
    for p in range(3):
        drain(ras[p], pas.at[p])
        drain(rbs[p], pbs.at[p])
        drain(rcs[p], p2s.at[p])
        drain(rds[p], p3s.at[p])
    drain(nra, nss.at[0])
    drain(nrb, nss.at[1])

    @pl.loop(0, 8)
    def _(q):
        _, _, same = weight_target(q)

        @pl.when(jnp.logical_not(same))
        def _():
            drain(wsend, ws.at[q])

        _, _, same_value = value_target(q)

        @pl.when(jnp.logical_not(same_value))
        def _():
            drain(vs.at[q], vss.at[q])

    @pl.loop(0, 4)
    def _(yb):
        _, _, dst, same = hidden_target(yb)

        @pl.when(jnp.logical_not(same))
        def _():
            drain(dst, hs.at[yb])

    drain(nmr, osend.at[0])
    drain(hbuf.at[rows_here], hfs.at[0])


def scratch():
    v, sem = pltpu.VMEM, pltpu.SemaphoreType.DMA
    sizes = [size for _, size in PARTS]
    return [
        v((4, 1024, 2048), BF16), v((2, 512, 512), BF16), v((512, 1024), BF16),
        *[v((4, 4, 4, n, 128), BF16) for n in sizes],
        *[v((4, 2, 2, n, 128), BF16) for n in sizes],
        *[v((4, 2, 4, n, 128), BF16) for n in sizes],
        *[v((4, 4, n, 128), BF16) for n in sizes],
        *[v((4, 3, n, 128), BF16) for n in sizes],
        *[v((4, n, 128), BF16) for n in sizes],
        *[v((3, n, 128), BF16) for n in sizes],
        v((3, 128, 512), F32), v((512, 128), F32), v((2, 8, 128), F32), v((7, 8, 128), F32), v((15, 8, 128), F32),
        v((128, 512), F32), v((64, 512), F32), v((128, 512), BF16), v((1024, 512), BF16),
        v((8, 128, 128), BF16), v((8, 128, 128), BF16),
        v((32, 512, 128), BF16), v((32, 512, 128), BF16), v((4, 32, 1024), BF16), v((4, 32, 128), BF16), v((256, 1024), BF16),
        v((1024, 128), F32), v((256, 128), F32), v((1024, 128), F32), v((1024, 128), F32), v((32, 32, 128), F32), v((32, 32, 128), F32),
        sem((13,)), sem((4,)), sem((4,)), sem((4,)), sem((4,)),
        sem((3,)), sem((4, 3)), sem((3,)), sem((4, 3)), sem((3,)), sem((4, 3)), sem((3,)), sem((3,)),
        sem((2,)), sem((2,)), sem((8,)), sem((1,)), sem((4,)), sem((1,)), sem((1,)), sem((1,)), sem((8,)), sem((1,)), sem((1,)), sem((1,)),
    ]


def on_device(
    acts, cotangent, master, moment1, moment2, hidden_in, k_cache, v_cache, k_new, queries, cache_len
):
    place = pl.BlockSpec(memory_space=pl.ANY)
    new_master, out = pl.pallas_call(
        kernel,
        name="update_and_decode",
        out_shape=(jax.ShapeDtypeStruct((64, 1024), F32), jax.ShapeDtypeStruct((4, 32, 1024), BF16)),
        in_specs=[pl.BlockSpec(memory_space=pltpu.SMEM)] + [place] * 10,
        out_specs=(pl.BlockSpec(memory_space=pltpu.VMEM), pl.BlockSpec(memory_space=pltpu.VMEM)),
        scratch_shapes=scratch(),
        compiler_params=pltpu.CompilerParams(
            collective_id=0, has_side_effects=True, vmem_limit_bytes=60 * 2**20
        ),
    )(
        cache_len[0], acts, cotangent, master, moment1, moment2, hidden_in.reshape(128, 1024),
        k_cache[0, 0], v_cache[0, 0], k_new[:, 0, 0], queries[:, 0, 0],
    )
    return new_master, out.reshape(4, 1, 1, 32, 1024)


def solution(mesh):
    rows = P(("fsdp", "dp"), None)
    in_specs = (
        rows, rows, rows, rows, rows,
        P(None, "dp", "fsdp", None, None),
        P("dp", "fsdp", None, None, None),
        P("dp", "fsdp", None, None, None),
        P(None, "dp", "fsdp", None, None),
        P(None, "dp", "fsdp", None, None),
        P("dp", None, None),
    )
    out_specs = (rows, P(None, "dp", "fsdp", None, None))
    return jax.shard_map(on_device, mesh=mesh, in_specs=in_specs, out_specs=out_specs, check_vma=False)
```

```python
import functools

import jax
import jax.numpy as jnp
from jax import lax
from jax.experimental import pallas as pl
from jax.experimental.pallas import tpu as pltpu
from jax.sharding import PartitionSpec as P

MESH = pl.DeviceIdType.MESH
F32 = jnp.float32
BF16 = jnp.bfloat16
PARTS = ((0, 176), (176, 176), (352, 160))
NT = (((1,), (1,)), ((), ()))


def coordinates():
    f, d = lax.axis_index("fsdp"), lax.axis_index("dp")
    return ((f // 4) % 4, f % 4, (d // 2) * 2 + f // 16), d % 2


def device(pos, core):
    x, y, z = pos
    return ((z % 2) * 16 + x * 4 + y, (z // 2) * 2 + core)


def shifted(pos, dim, delta):
    return tuple((v + delta) % 4 if i == dim else v for i, v in enumerate(pos))


def kernel(
    lens, acts, cot, master, mom1, mom2, hid, keys, vals, knew, query,
    nm_out, at_out,
    abuf, cbuf, ct, g0, g1, g2, ra0, ra1, ra2, rb0, rb1, rb2, s0, s1, s2, rc0, rc1, rc2, t0, t1, t2, rd0, rd1, rd2,
    ms, gt, nsend, nra, nrb, nmx, nmr, wsend, wbuf, vs, vr,
    kbuf, vbuf, qbuf, knbuf, hbuf, qs, kns, acc, ens, accn, enn,
    loc, asend, arecv, xsend, xrecv, pas, par, pbs, pbr, p2s, p2r, p3s, p3r, nss, nsr, ws, wr, hs, hr, hfs, hfr, vss, vsr, osend, orecv,
):
    pos, core = coordinates()
    x, y, z = pos
    other = 1 - core
    me = device(pos, core)
    sib = device(pos, other)
    gs, ras, rbs, ss, rcs, ts, rds = (
        (g0, g1, g2), (ra0, ra1, ra2), (rb0, rb1, rb2), (s0, s1, s2), (rc0, rc1, rc2), (t0, t1, t2), (rd0, rd1, rd2)
    )

    def copy(src, dst, sem):
        return pltpu.make_async_copy(src, dst, sem)

    def remote(src, dst, ssem, rsem, dev):
        return pltpu.make_async_remote_copy(
            src_ref=src, dst_ref=dst, send_sem=ssem, recv_sem=rsem, device_id=dev, device_id_type=MESH
        )

    def drain(ref, sem):
        pltpu.make_async_copy(ref, ref, sem).wait()

    def lanes(k, j):
        xb, yb = j // 4, j % 4
        zb = (k + 8 - xb - yb) % 4
        return pl.ds(pl.multiple_of((((zb % 2) * 16 + xb * 4 + yb) * 2 + zb // 2) * 128, 128), 128)

    half = pl.ds(pl.multiple_of(core * 512, 512), 512)
    far = pl.ds(pl.multiple_of(other * 512, 512), 512)
    mine = pl.ds(pl.multiple_of(core * 64, 64), 64)
    theirs = pl.ds(pl.multiple_of(other * 64, 64), 64)

    tokens_here = pl.ds(pl.multiple_of(core * 256, 256), 256)
    tokens_there = pl.ds(pl.multiple_of(other * 256, 256), 256)

    def hidden_target(yb):
        src = hid.at[:, pl.ds(pl.multiple_of(yb * 256, 256), 256)]
        dst = hbuf.at[
            pl.ds(pl.multiple_of(core * 256 + (x // 2) * 128, 128), 128),
            pl.ds(pl.multiple_of((x % 2) * 256, 256), 256),
        ]
        return (y, yb, z), src, dst, (y == x) & (yb == y)

    barrier = pltpu.get_barrier_semaphore()
    pl.semaphore_signal(barrier, inc=1, device_id=sib, device_id_type=MESH)
    for dim in range(3):
        for delta in (1, 2, 3):
            pl.semaphore_signal(barrier, inc=1, device_id=device(shifted(pos, dim, delta), core), device_id_type=MESH)

    copy(cot.at[:, half], cbuf.at[0], loc.at[4]).start()
    for k in range(4):
        @pl.loop(0, 16)
        def _(j):
            to = pl.ds(pl.multiple_of(j * 128, 128), 128)
            copy(acts.at[:, lanes(k, j)], abuf.at[k, pl.ds(0, 512), to], loc.at[k]).start()

    copy(query, qbuf, loc.at[6]).start()
    copy(knew, knbuf, loc.at[7]).start()
    copy(keys, kbuf, loc.at[8]).start()
    copy(vals, vbuf, loc.at[9]).start()
    for i, ref in enumerate((master, mom1, mom2)):
        copy(ref.at[:, half], ms.at[i, mine], loc.at[10 + i]).start()
    pl.semaphore_wait(barrier, 10)

    remote(cot.at[:, far], cbuf.at[1], xsend.at[0], xrecv.at[0], sib).start()
    for k in range(4):
        @pl.loop(0, 16)
        def _(j):
            to = pl.ds(pl.multiple_of(j * 128, 128), 128)
            remote(acts.at[:, lanes(k, j)], abuf.at[k, pl.ds(512, 512), to], asend.at[k], arecv.at[k, j // 4], sib).start()

    for i, ref in enumerate((master, mom1, mom2)):
        remote(ref.at[:, far], ms.at[i, mine], xsend.at[1 + i], xrecv.at[1 + i], sib).start()

    copy(cot.at[:, half], cbuf.at[0], loc.at[4]).wait()
    ct[:, 0:512] = cbuf[0].T
    drain(cbuf.at[1], xrecv.at[0])
    ct[:, 512:1024] = cbuf[1].T

    def pass_on(k):
        for p in range(3):
            g, ra, rb = gs[p], ras[p], rbs[p]
            up, down = shifted(pos, p, 1), shifted(pos, p, 3)
            drain(ra.at[k], par.at[k, p])

            @pl.loop(0, 2)
            def _(i):
                g[k, up[p], i] = (g[k, up[p], i].astype(F32) + ra[k, 0, i].astype(F32)).astype(BF16)
                g[k, down[p], 2 + i] = (g[k, down[p], 2 + i].astype(F32) + ra[k, 1, i].astype(F32)).astype(BF16)

            remote(g.at[k, up[p], 0:2], rb.at[k, 0, 0:2], pbs.at[p], pbr.at[k, p], device(up, core)).start()
            remote(g.at[k, down[p], 2:4], rb.at[k, 1, 2:4], pbs.at[p], pbr.at[k, p], device(down, core)).start()

    for k in range(4):
        drain(abuf.at[k, pl.ds(0, 512)], loc.at[k])
        @pl.loop(0, 4)
        def _(xb):
            cols = pl.ds(pl.multiple_of(xb * 512, 512), 512)
            drain(abuf.at[k, pl.ds(512, 512), cols], arecv.at[k, xb])
            res = jnp.dot(ct[...], abuf[k, :, cols], preferred_element_type=F32).astype(BF16)
            for yb in range(4):
                zb = (k + 8 - xb - yb) % 4
                piece = res[:, yb * 128 : (yb + 1) * 128]
                g0[k, xb, yb] = piece[0:176]
                g1[k, yb, zb] = piece[176:352]
                g2[k, zb, xb] = piece[352:512]

        for p in range(3):
            g, ra, rb = gs[p], ras[p], rbs[p]
            up, down, opposite = shifted(pos, p, 1), shifted(pos, p, 3), (pos[p] + 2) % 4
            to_up, to_down = device(up, core), device(down, core)
            remote(g.at[k, opposite, 0:2], ra.at[k, 0], pas.at[p], par.at[k, p], to_up).start()
            remote(g.at[k, opposite, 2:4], ra.at[k, 1], pas.at[p], par.at[k, p], to_down).start()
            remote(g.at[k, up[p], 2:4], rb.at[k, 0, 2:4], pbs.at[p], pbr.at[k, p], to_up).start()
            remote(g.at[k, down[p], 0:2], rb.at[k, 1, 0:2], pbs.at[p], pbr.at[k, p], to_down).start()
        if k > 0:
            pass_on(k - 1)


    copy(query, qbuf, loc.at[6]).wait()
    copy(knew, knbuf, loc.at[7]).wait()
    for s in range(4):
        for h in range(8):
            qs[pl.ds(s * 8 + h, 32, stride=32), :] = qbuf[s, :, h * 128 : (h + 1) * 128].astype(F32)
    kns[...] = jnp.zeros_like(kns)
    for s in range(4):
        kns[pl.ds(s, 32, stride=8), :] = knbuf[s].astype(F32)
    copy(keys, kbuf, loc.at[8]).wait()
    copy(vals, vbuf, loc.at[9]).wait()
    replica = (z % 2) * 2 + x // 2
    scale = 128 ** (-0.5)

    def attend(i):
        rows = pl.ds(pl.multiple_of(i * 32, 32), 32)
        qi = qs[rows, :].astype(BF16)
        sc = lax.dot_general(qi, kbuf[i], NT, preferred_element_type=F32) * scale
        slot = lax.broadcasted_iota(jnp.int32, (32, 512), 1)
        sc = jnp.where(slot < lens[replica, i], sc, -1e30)
        kn = kns[pl.ds(pl.multiple_of(i * 8, 8), 8), :].astype(BF16)
        sn = lax.dot_general(qi, kn, NT, preferred_element_type=F32) * scale
        step = lax.broadcasted_iota(jnp.int32, (32, 8), 0) // 8
        sn = jnp.where(lax.broadcasted_iota(jnp.int32, (32, 8), 1) <= step, sn, -1e30)
        top = jnp.maximum(jnp.max(sc, 1, keepdims=True), jnp.max(sn, 1, keepdims=True))
        ec = jnp.exp(sc - top)
        en = jnp.exp(sn - top)
        inv = 1.0 / (jnp.sum(ec, 1, keepdims=True) + jnp.sum(en, 1, keepdims=True))
        out = jnp.dot(ec.astype(BF16), vbuf[i], preferred_element_type=F32)
        acc[rows, :] = out * inv
        ens[rows, 0:8] = en.astype(BF16).astype(F32) * inv

    def attend_rows(first, pairs=4):
        @pl.loop(0, pairs)
        def _(i):
            attend(first + 2 * i)
            attend(first + 2 * i + 1)

    def first_sum(k):
        for p in range(3):
            b = (p + 1) % 3
            drain(rbs[p].at[k], pbr.at[k, p])

            @pl.loop(0, 4)
            def _(i):
                total = gs[p][k, pos[p], i].astype(F32) + rbs[p][k, 0, i].astype(F32) + rbs[p][k, 1, i].astype(F32)
                ss[p][k, i] = total.astype(BF16)

            for delta in (1, 2, 3):
                to = shifted(pos, b, delta)
                remote(
                    ss[p].at[k, to[b]], rcs[p].at[k, delta - 1], p2s.at[p], p2r.at[k, p], device(to, core)
                ).start()

    def second_sum(k):
        for p in range(3):
            b, c = (p + 1) % 3, (p + 2) % 3
            drain(rcs[p].at[k], p2r.at[k, p])
            total = ss[p][k, pos[b]].astype(F32)
            for slot in range(3):
                total += rcs[p][k, slot].astype(F32)
            ts[p][k] = total.astype(BF16)
            target = (k + 8 - pos[p] - pos[b]) % 4
            delta = (target + 4 - pos[c]) % 4

            @pl.when(delta != 0)
            def _():
                remote(
                    ts[p].at[k], rds[p].at[delta - 1], p3s.at[p], p3r.at[p], device(shifted(pos, c, delta), core)
                ).start()

    attend_rows(0, 2)
    pass_on(3)
    attend_rows(4, 2)
    first_sum(0)
    attend_rows(8)
    first_sum(1)
    second_sum(0)
    attend_rows(16)
    first_sum(2)
    second_sum(1)
    first_sum(3)
    second_sum(2)
    second_sum(3)

    own = (x + y + z) % 4
    for p, (first, size) in enumerate(PARTS):
        drain(rds[p], p3r.at[p])
        total = ts[p][own].astype(F32)
        for slot in range(3):
            total += rds[p][slot].astype(F32)
        gt[pl.ds(first, size), :] = total

    square = jnp.zeros((8, 128), F32)
    for i in range(64):
        part = gt[pl.ds(i * 8, 8), :]
        square += part * part
    nsend[0] = square
    for q in range(1, 8):
        to = device(((x + q // 2) % 4, y, z), (core + q) % 2)
        remote(nsend.at[0], nra.at[q - 1], nss.at[0], nsr.at[0], to).start()
    attend_rows(24, 2)
    drain(nra, nsr.at[0])
    for slot in range(7):
        square += nra[slot]
    nsend[1] = square
    for q in range(1, 16):
        to = device((x, (y + q // 4) % 4, (z + q) % 4), core)
        remote(nsend.at[1], nrb.at[q - 1], nss.at[1], nsr.at[1], to).start()
    @pl.loop(0, 4)
    def _(yb):
        to, src, dst, same = hidden_target(yb)

        @pl.when(jnp.logical_not(same))
        def _():
            remote(src, dst, hs.at[yb], hr.at[0], device(to, core)).start()

        @pl.when(same)
        def _():
            copy(src, dst, hr.at[0]).start()

    attend_rows(28, 2)
    for j in range(32):
        accn[j] = acc[pl.ds(j, 32, stride=32), :]
        enn[j] = ens[pl.ds(j, 32, stride=32), :]
    drain(nrb, nsr.at[1])
    for slot in range(15):
        square += nrb[slot]
    gnorm = jnp.sqrt(jnp.sum(square, keepdims=True))
    clip = jnp.minimum(1.0, 1.0 / (gnorm + 1e-06))

    for i in range(3):
        drain(ms.at[i, mine], loc.at[10 + i])
        drain(ms.at[i, theirs], xrecv.at[1 + i])
    place = pl.ds(pl.multiple_of(((z % 2) * 2 + z // 2) * 128, 128), 128)
    for j in range(4):
        cols = slice(j * 128, (j + 1) * 128)
        clipped = gt[pl.ds(j * 128, 128), :].T * clip
        mom = 0.9 * ms[1, :, cols] + 0.1 * clipped
        sec = 0.95 * ms[2, :, cols] + 0.05 * clipped * clipped
        update = mom / (1.0 - 0.9**10) / (jnp.sqrt(sec / (1.0 - 0.95**10)) + 1e-08)
        weights = ms[0, :, cols]
        weights = weights - 0.1 * (update + 0.1 * weights)
        nmx[:, cols] = weights
        wsend[j] = weights.astype(BF16)
        for q in (2, 1, 3):
            to = (x, y, (z + q) % 4)
            remote(wsend.at[j], wbuf.at[j, place], ws.at[0], wr.at[j], device(to, core)).start()
        copy(wsend.at[j], wbuf.at[j, place], wr.at[j]).start()

    drain(hbuf.at[tokens_here], hr.at[0])
    remote(hbuf.at[tokens_here], hbuf.at[tokens_here], hfs.at[0], hfr.at[0], sib).start()
    remote(nmx.at[theirs], nmr, osend.at[0], orecv.at[0], sib).start()
    nm_out[:, half] = nmx[mine, :]
    drain(hbuf.at[tokens_there], hfr.at[0])
    drain(nmr, orecv.at[0])
    nm_out[:, far] = nmr[...]

    number = x * 4 + y
    for j in range(4):
        drain(wbuf.at[j], wr.at[j])
        res = jnp.dot(hbuf[...], wbuf[j], preferred_element_type=F32).astype(BF16)
        for xp in range(2):
            for c in range(2):
                q = j * 4 + xp * 2 + c
                vs[q] = res[c * 256 + xp * 128 : c * 256 + (xp + 1) * 128]
                to = (xp * 2 + core, j, z)
                same = (to[0] == x) & (to[1] == y) & (c == core)

                @pl.when(jnp.logical_not(same))
                def _():
                    remote(vs.at[q], vr.at[number], vss.at[q], vsr.at[0], device(to, c)).start()

                @pl.when(same)
                def _():
                    copy(vs.at[q], vr.at[number], vsr.at[0]).start()

    drain(vr, vsr.at[0])
    total = vr[0].astype(F32)
    for slot in range(1, 16):
        total += vr[slot].astype(F32)
    vnew = (total * (32.0 * 8192 ** (-0.5))).astype(BF16).astype(F32)
    for s in range(4):
        for h in range(8):
            out = accn[s * 8 + h]
            weight = enn[s * 8 + h]
            for t in range(s + 1):
                out += weight[:, t : t + 1] * vnew[t * 32 : (t + 1) * 32]
            at_out[s, :, h * 128 : (h + 1) * 128] = out.astype(BF16)

    drain(cbuf.at[1], xsend.at[0])
    for i in range(3):
        drain(ms.at[i, theirs], xsend.at[1 + i])
    for k in range(4):
        drain(abuf.at[k, pl.ds(512, 512)], asend.at[k])
    for p in range(3):
        drain(ras[p], pas.at[p])
        drain(rbs[p], pbs.at[p])
        drain(rcs[p], p2s.at[p])
        drain(rds[p], p3s.at[p])
    drain(nra, nss.at[0])
    drain(nrb, nss.at[1])

    drain(wbuf.at[:, pl.ds(0, 384)], ws.at[0])

    @pl.loop(0, 16)
    def _(q):
        same = ((q // 2) % 2 * 2 + core == x) & (q // 4 == y) & (q % 2 == core)

        @pl.when(jnp.logical_not(same))
        def _():
            drain(vs.at[q], vss.at[q])

    @pl.loop(0, 4)
    def _(yb):
        _, _, dst, same = hidden_target(yb)

        @pl.when(jnp.logical_not(same))
        def _():
            drain(dst, hs.at[yb])

    drain(nmr, osend.at[0])
    drain(hbuf.at[tokens_here], hfs.at[0])


def scratch():
    v, sem = pltpu.VMEM, pltpu.SemaphoreType.DMA
    sizes = [size for _, size in PARTS]
    return [
        v((4, 1024, 2048), BF16), v((2, 512, 512), BF16), v((512, 1024), BF16),
        *[v((4, 4, 4, n, 128), BF16) for n in sizes],
        *[v((4, 2, 2, n, 128), BF16) for n in sizes],
        *[v((4, 2, 4, n, 128), BF16) for n in sizes],
        *[v((4, 4, n, 128), BF16) for n in sizes],
        *[v((4, 3, n, 128), BF16) for n in sizes],
        *[v((4, n, 128), BF16) for n in sizes],
        *[v((3, n, 128), BF16) for n in sizes],
        v((3, 128, 512), F32), v((512, 128), F32), v((2, 8, 128), F32), v((7, 8, 128), F32), v((15, 8, 128), F32),
        v((128, 512), F32), v((64, 512), F32), v((4, 128, 128), BF16), v((4, 512, 128), BF16),
        v((16, 128, 128), BF16), v((16, 128, 128), BF16),
        v((32, 512, 128), BF16), v((32, 512, 128), BF16), v((4, 32, 1024), BF16), v((4, 32, 128), BF16), v((512, 512), BF16),
        v((1024, 128), F32), v((256, 128), F32), v((1024, 128), F32), v((1024, 128), F32), v((32, 32, 128), F32), v((32, 32, 128), F32),
        sem((13,)), sem((4,)), sem((4, 4)), sem((4,)), sem((4,)),
        sem((3,)), sem((4, 3)), sem((3,)), sem((4, 3)), sem((3,)), sem((4, 3)), sem((3,)), sem((3,)),
        sem((2,)), sem((2,)), sem((1,)), sem((4,)), sem((4,)), sem((1,)), sem((1,)), sem((1,)), sem((16,)), sem((1,)), sem((1,)), sem((1,)),
    ]


def on_device(
    acts, cotangent, master, moment1, moment2, hidden_in, k_cache, v_cache, k_new, queries, cache_len
):
    place = pl.BlockSpec(memory_space=pl.ANY)
    new_master, out = pl.pallas_call(
        kernel,
        name="update_and_decode",
        out_shape=(jax.ShapeDtypeStruct((64, 1024), F32), jax.ShapeDtypeStruct((4, 32, 1024), BF16)),
        in_specs=[pl.BlockSpec(memory_space=pltpu.SMEM)] + [place] * 10,
        out_specs=(pl.BlockSpec(memory_space=pltpu.VMEM), pl.BlockSpec(memory_space=pltpu.VMEM)),
        scratch_shapes=scratch(),
        compiler_params=pltpu.CompilerParams(
            collective_id=0, has_side_effects=True, vmem_limit_bytes=60 * 2**20
        ),
    )(
        cache_len[0], acts, cotangent, master, moment1, moment2, hidden_in.reshape(128, 1024),
        k_cache[0, 0], v_cache[0, 0], k_new[:, 0, 0], queries[:, 0, 0],
    )
    return new_master, out.reshape(4, 1, 1, 32, 1024)


def solution(mesh):
    rows = P(("fsdp", "dp"), None)
    in_specs = (
        rows, rows, rows, rows, rows,
        P(None, "dp", "fsdp", None, None),
        P("dp", "fsdp", None, None, None),
        P("dp", "fsdp", None, None, None),
        P(None, "dp", "fsdp", None, None),
        P(None, "dp", "fsdp", None, None),
        P("dp", None, None),
    )
    out_specs = (rows, P(None, "dp", "fsdp", None, None))
    return jax.shard_map(on_device, mesh=mesh, in_specs=in_specs, out_specs=out_specs, check_vma=False)
```

```python
import functools

import jax
import jax.numpy as jnp
from jax import lax
from jax.experimental import pallas as pl
from jax.experimental.pallas import tpu as pltpu
from jax.sharding import PartitionSpec as P

MESH = pl.DeviceIdType.MESH
F32 = jnp.float32
BF16 = jnp.bfloat16
PARTS = ((0, 176), (176, 176), (352, 160))
NT = (((1,), (1,)), ((), ()))


def coordinates():
    f, d = lax.axis_index("fsdp"), lax.axis_index("dp")
    return ((f // 4) % 4, f % 4, (d // 2) * 2 + f // 16), d % 2


def device(pos, core):
    x, y, z = pos
    return ((z % 2) * 16 + x * 4 + y, (z // 2) * 2 + core)


def shifted(pos, dim, delta):
    return tuple((v + delta) % 4 if i == dim else v for i, v in enumerate(pos))


def kernel(
    lens, acts, cot, master, mom1, mom2, hid, keys, vals, knew, query,
    nm_out, at_out,
    abuf, cbuf, ct, g0, g1, g2, ra0, ra1, ra2, rb0, rb1, rb2, s0, s1, s2, rc0, rc1, rc2, t0, t1, t2, rd0, rd1, rd2,
    ms, gt, nsend, nra, nrb, nmx, nmr, wsend, wbuf, vs, vr,
    kbuf, vbuf, qbuf, knbuf, hbuf, qs, kns, acc, ens, accn, enn,
    loc, asend, arecv, xsend, xrecv, pas, par, pbs, pbr, p2s, p2r, p3s, p3r, nss, nsr, ws, wr, hs, hr, hfs, hfr, vss, vsr, osend, orecv,
):
    pos, core = coordinates()
    x, y, z = pos
    other = 1 - core
    me = device(pos, core)
    sib = device(pos, other)
    gs, ras, rbs, ss, rcs, ts, rds = (
        (g0, g1, g2), (ra0, ra1, ra2), (rb0, rb1, rb2), (s0, s1, s2), (rc0, rc1, rc2), (t0, t1, t2), (rd0, rd1, rd2)
    )

    def copy(src, dst, sem):
        return pltpu.make_async_copy(src, dst, sem)

    def remote(src, dst, ssem, rsem, dev):
        return pltpu.make_async_remote_copy(
            src_ref=src, dst_ref=dst, send_sem=ssem, recv_sem=rsem, device_id=dev, device_id_type=MESH
        )

    def drain(ref, sem):
        pltpu.make_async_copy(ref, ref, sem).wait()

    def lanes(k, j):
        xb, yb = j // 4, j % 4
        zb = (k + 8 - xb - yb) % 4
        return pl.ds(pl.multiple_of((((zb % 2) * 16 + xb * 4 + yb) * 2 + zb // 2) * 128, 128), 128)

    half = pl.ds(pl.multiple_of(core * 512, 512), 512)
    far = pl.ds(pl.multiple_of(other * 512, 512), 512)
    mine = pl.ds(pl.multiple_of(core * 64, 64), 64)
    theirs = pl.ds(pl.multiple_of(other * 64, 64), 64)

    tokens_here = pl.ds(pl.multiple_of(core * 256, 256), 256)
    tokens_there = pl.ds(pl.multiple_of(other * 256, 256), 256)

    def hidden_target(yb):
        src = hid.at[:, pl.ds(pl.multiple_of(yb * 256, 256), 256)]
        dst = hbuf.at[
            pl.ds(pl.multiple_of(core * 256 + (x // 2) * 128, 128), 128),
            pl.ds(pl.multiple_of((x % 2) * 256, 256), 256),
        ]
        return (y, yb, z), src, dst, (y == x) & (yb == y)

    barrier = pltpu.get_barrier_semaphore()
    pl.semaphore_signal(barrier, inc=1, device_id=sib, device_id_type=MESH)
    for dim in (2, 1, 0):
        for delta in (2, 1, 3):
            pl.semaphore_signal(barrier, inc=1, device_id=device(shifted(pos, dim, delta), core), device_id_type=MESH)

    copy(cot.at[:, half], cbuf.at[0], loc.at[4]).start()
    for k in range(4):
        @pl.loop(0, 16)
        def _(j):
            to = pl.ds(pl.multiple_of(j * 128, 128), 128)
            copy(acts.at[:, lanes(k, j)], abuf.at[k, pl.ds(0, 512), to], loc.at[k]).start()

    copy(query, qbuf, loc.at[6]).start()
    copy(knew, knbuf, loc.at[7]).start()
    copy(keys, kbuf, loc.at[8]).start()
    copy(vals, vbuf, loc.at[9]).start()
    for i, ref in enumerate((master, mom1, mom2)):
        copy(ref.at[:, half], ms.at[i, mine], loc.at[10 + i]).start()
    pl.semaphore_wait(barrier, 10)

    remote(cot.at[:, far], cbuf.at[1], xsend.at[0], xrecv.at[0], sib).start()
    for k in range(4):
        @pl.loop(0, 16)
        def _(j):
            to = pl.ds(pl.multiple_of(j * 128, 128), 128)
            remote(acts.at[:, lanes(k, j)], abuf.at[k, pl.ds(512, 512), to], asend.at[k], arecv.at[k, j // 4], sib).start()

    for i, ref in enumerate((master, mom1, mom2)):
        remote(ref.at[:, far], ms.at[i, mine], xsend.at[1 + i], xrecv.at[1 + i], sib).start()

    copy(cot.at[:, half], cbuf.at[0], loc.at[4]).wait()
    ct[:, 0:512] = cbuf[0].T
    drain(cbuf.at[1], xrecv.at[0])
    ct[:, 512:1024] = cbuf[1].T

    def pass_on(k):
        for p in range(3):
            g, ra, rb = gs[p], ras[p], rbs[p]
            up, down = shifted(pos, p, 1), shifted(pos, p, 3)
            drain(ra.at[k], par.at[k, p])

            @pl.loop(0, 2)
            def _(i):
                g[k, up[p], i] = (g[k, up[p], i].astype(F32) + ra[k, 0, i].astype(F32)).astype(BF16)
                g[k, down[p], 2 + i] = (g[k, down[p], 2 + i].astype(F32) + ra[k, 1, i].astype(F32)).astype(BF16)

            remote(g.at[k, up[p], 0:2], rb.at[k, 0, 0:2], pbs.at[p], pbr.at[k, p], device(up, core)).start()
            remote(g.at[k, down[p], 2:4], rb.at[k, 1, 2:4], pbs.at[p], pbr.at[k, p], device(down, core)).start()

    for k in range(4):
        drain(abuf.at[k, pl.ds(0, 512)], loc.at[k])
        @pl.loop(0, 4)
        def _(xb):
            cols = pl.ds(pl.multiple_of(xb * 512, 512), 512)
            drain(abuf.at[k, pl.ds(512, 512), cols], arecv.at[k, xb])
            res = jnp.dot(ct[...], abuf[k, :, cols], preferred_element_type=F32).astype(BF16)
            for yb in range(4):
                zb = (k + 8 - xb - yb) % 4
                piece = res[:, yb * 128 : (yb + 1) * 128]
                g0[k, xb, yb] = piece[0:176]
                g1[k, yb, zb] = piece[176:352]
                g2[k, zb, xb] = piece[352:512]

        for p in range(3):
            g, ra, rb = gs[p], ras[p], rbs[p]
            up, down, opposite = shifted(pos, p, 1), shifted(pos, p, 3), (pos[p] + 2) % 4
            to_up, to_down = device(up, core), device(down, core)
            remote(g.at[k, opposite, 0:2], ra.at[k, 0], pas.at[p], par.at[k, p], to_up).start()
            remote(g.at[k, opposite, 2:4], ra.at[k, 1], pas.at[p], par.at[k, p], to_down).start()
            remote(g.at[k, up[p], 2:4], rb.at[k, 0, 2:4], pbs.at[p], pbr.at[k, p], to_up).start()
            remote(g.at[k, down[p], 0:2], rb.at[k, 1, 0:2], pbs.at[p], pbr.at[k, p], to_down).start()
        if k > 0:
            pass_on(k - 1)


    copy(query, qbuf, loc.at[6]).wait()
    copy(knew, knbuf, loc.at[7]).wait()
    for s in range(4):
        for h in range(8):
            qs[pl.ds(s * 8 + h, 32, stride=32), :] = qbuf[s, :, h * 128 : (h + 1) * 128].astype(F32)
    kns[...] = jnp.zeros_like(kns)
    for s in range(4):
        kns[pl.ds(s, 32, stride=8), :] = knbuf[s].astype(F32)
    copy(keys, kbuf, loc.at[8]).wait()
    copy(vals, vbuf, loc.at[9]).wait()
    replica = (z % 2) * 2 + x // 2
    scale = 128 ** (-0.5)

    def attend(i):
        rows = pl.ds(pl.multiple_of(i * 32, 32), 32)
        qi = qs[rows, :].astype(BF16)
        sc = lax.dot_general(qi, kbuf[i], NT, preferred_element_type=F32) * scale
        slot = lax.broadcasted_iota(jnp.int32, (32, 512), 1)
        sc = jnp.where(slot < lens[replica, i], sc, -1e30)
        kn = kns[pl.ds(pl.multiple_of(i * 8, 8), 8), :].astype(BF16)
        sn = lax.dot_general(qi, kn, NT, preferred_element_type=F32) * scale
        step = lax.broadcasted_iota(jnp.int32, (32, 8), 0) // 8
        sn = jnp.where(lax.broadcasted_iota(jnp.int32, (32, 8), 1) <= step, sn, -1e30)
        top = jnp.maximum(jnp.max(sc, 1, keepdims=True), jnp.max(sn, 1, keepdims=True))
        ec = jnp.exp(sc - top)
        en = jnp.exp(sn - top)
        inv = 1.0 / (jnp.sum(ec, 1, keepdims=True) + jnp.sum(en, 1, keepdims=True))
        out = jnp.dot(ec.astype(BF16), vbuf[i], preferred_element_type=F32)
        acc[rows, :] = out * inv
        ens[rows, 0:8] = en.astype(BF16).astype(F32) * inv

    def attend_rows(first, pairs=4):
        @pl.loop(0, pairs)
        def _(i):
            attend(first + 2 * i)
            attend(first + 2 * i + 1)

    def first_sum(k):
        for p in range(3):
            b = (p + 1) % 3
            drain(rbs[p].at[k], pbr.at[k, p])

            @pl.loop(0, 4)
            def _(i):
                total = gs[p][k, pos[p], i].astype(F32) + rbs[p][k, 0, i].astype(F32) + rbs[p][k, 1, i].astype(F32)
                ss[p][k, i] = total.astype(BF16)

            for delta in (1, 2, 3):
                to = shifted(pos, b, delta)
                remote(
                    ss[p].at[k, to[b]], rcs[p].at[k, delta - 1], p2s.at[p], p2r.at[k, p], device(to, core)
                ).start()

    def second_sum(k):
        for p in range(3):
            b, c = (p + 1) % 3, (p + 2) % 3
            drain(rcs[p].at[k], p2r.at[k, p])
            total = ss[p][k, pos[b]].astype(F32)
            for slot in range(3):
                total += rcs[p][k, slot].astype(F32)
            ts[p][k] = total.astype(BF16)
            target = (k + 8 - pos[p] - pos[b]) % 4
            delta = (target + 4 - pos[c]) % 4

            @pl.when(delta != 0)
            def _():
                remote(
                    ts[p].at[k], rds[p].at[delta - 1], p3s.at[p], p3r.at[p], device(shifted(pos, c, delta), core)
                ).start()

    attend_rows(0, 2)
    pass_on(3)
    attend_rows(4, 2)
    first_sum(0)
    attend_rows(8)
    first_sum(1)
    second_sum(0)
    first_sum(2)
    second_sum(1)
    first_sum(3)
    second_sum(2)
    second_sum(3)

    own = (x + y + z) % 4
    for p, (first, size) in enumerate(PARTS):
        drain(rds[p], p3r.at[p])
        total = ts[p][own].astype(F32)
        for slot in range(3):
            total += rds[p][slot].astype(F32)
        gt[pl.ds(first, size), :] = total

    square = jnp.zeros((8, 128), F32)
    for i in range(64):
        part = gt[pl.ds(i * 8, 8), :]
        square += part * part
    nsend[0] = square
    for q in range(1, 8):
        to = device(((x + q // 2) % 4, y, z), (core + q) % 2)
        remote(nsend.at[0], nra.at[q - 1], nss.at[0], nsr.at[0], to).start()
    attend_rows(16, 4)
    drain(nra, nsr.at[0])
    for slot in range(7):
        square += nra[slot]
    nsend[1] = square
    for q in range(1, 16):
        to = device((x, (y + q // 4) % 4, (z + q) % 4), core)
        remote(nsend.at[1], nrb.at[q - 1], nss.at[1], nsr.at[1], to).start()
    @pl.loop(0, 4)
    def _(yb):
        to, src, dst, same = hidden_target(yb)

        @pl.when(jnp.logical_not(same))
        def _():
            remote(src, dst, hs.at[yb], hr.at[0], device(to, core)).start()

        @pl.when(same)
        def _():
            copy(src, dst, hr.at[0]).start()

    attend_rows(24, 4)
    for j in range(32):
        accn[j] = acc[pl.ds(j, 32, stride=32), :]
        enn[j] = ens[pl.ds(j, 32, stride=32), :]
    drain(nrb, nsr.at[1])
    for slot in range(15):
        square += nrb[slot]
    gnorm = jnp.sqrt(jnp.sum(square, keepdims=True))
    clip = jnp.minimum(1.0, 1.0 / (gnorm + 1e-06))

    for i in range(3):
        drain(ms.at[i, mine], loc.at[10 + i])
        drain(ms.at[i, theirs], xrecv.at[1 + i])
    place = pl.ds(pl.multiple_of(((z % 2) * 2 + z // 2) * 128, 128), 128)
    for j in range(4):
        cols = slice(j * 128, (j + 1) * 128)
        clipped = gt[pl.ds(j * 128, 128), :].T * clip
        mom = 0.9 * ms[1, :, cols] + 0.1 * clipped
        sec = 0.95 * ms[2, :, cols] + 0.05 * clipped * clipped
        update = mom / (1.0 - 0.9**10) / (jnp.sqrt(sec / (1.0 - 0.95**10)) + 1e-08)
        weights = ms[0, :, cols]
        weights = weights - 0.1 * (update + 0.1 * weights)
        nmx[:, cols] = weights
        wsend[j] = weights.astype(BF16)
        for q in (2, 1, 3):
            to = (x, y, (z + q) % 4)
            remote(wsend.at[j], wbuf.at[j, place], ws.at[0], wr.at[j], device(to, core)).start()
        copy(wsend.at[j], wbuf.at[j, place], wr.at[j]).start()

    drain(hbuf.at[tokens_here], hr.at[0])
    remote(hbuf.at[tokens_here], hbuf.at[tokens_here], hfs.at[0], hfr.at[0], sib).start()
    remote(nmx.at[theirs], nmr, osend.at[0], orecv.at[0], sib).start()
    nm_out[:, half] = nmx[mine, :]
    drain(hbuf.at[tokens_there], hfr.at[0])
    drain(nmr, orecv.at[0])
    nm_out[:, far] = nmr[...]

    number = x * 4 + y
    for j in range(4):
        drain(wbuf.at[j], wr.at[j])
        res = jnp.dot(hbuf[...], wbuf[j], preferred_element_type=F32).astype(BF16)
        for xp in range(2):
            for c in range(2):
                q = j * 4 + xp * 2 + c
                vs[q] = res[c * 256 + xp * 128 : c * 256 + (xp + 1) * 128]
                to = (xp * 2 + core, j, z)
                same = (to[0] == x) & (to[1] == y) & (c == core)

                @pl.when(jnp.logical_not(same))
                def _():
                    remote(vs.at[q], vr.at[number], vss.at[q], vsr.at[0], device(to, c)).start()

                @pl.when(same)
                def _():
                    copy(vs.at[q], vr.at[number], vsr.at[0]).start()

    drain(vr, vsr.at[0])
    total = vr[0].astype(F32)
    for slot in range(1, 16):
        total += vr[slot].astype(F32)
    vnew = (total * (32.0 * 8192 ** (-0.5))).astype(BF16).astype(F32)
    for s in range(4):
        for h in range(8):
            out = accn[s * 8 + h]
            weight = enn[s * 8 + h]
            for t in range(s + 1):
                out += weight[:, t : t + 1] * vnew[t * 32 : (t + 1) * 32]
            at_out[s, :, h * 128 : (h + 1) * 128] = out.astype(BF16)

    drain(cbuf.at[1], xsend.at[0])
    for i in range(3):
        drain(ms.at[i, theirs], xsend.at[1 + i])
    for k in range(4):
        drain(abuf.at[k, pl.ds(512, 512)], asend.at[k])
    for p in range(3):
        drain(ras[p], pas.at[p])
        drain(rbs[p], pbs.at[p])
        drain(rcs[p], p2s.at[p])
        drain(rds[p], p3s.at[p])
    drain(nra, nss.at[0])
    drain(nrb, nss.at[1])

    drain(wbuf.at[:, pl.ds(0, 384)], ws.at[0])

    @pl.loop(0, 16)
    def _(q):
        same = ((q // 2) % 2 * 2 + core == x) & (q // 4 == y) & (q % 2 == core)

        @pl.when(jnp.logical_not(same))
        def _():
            drain(vs.at[q], vss.at[q])

    @pl.loop(0, 4)
    def _(yb):
        _, _, dst, same = hidden_target(yb)

        @pl.when(jnp.logical_not(same))
        def _():
            drain(dst, hs.at[yb])

    drain(nmr, osend.at[0])
    drain(hbuf.at[tokens_here], hfs.at[0])


def scratch():
    v, sem = pltpu.VMEM, pltpu.SemaphoreType.DMA
    sizes = [size for _, size in PARTS]
    return [
        v((4, 1024, 2048), BF16), v((2, 512, 512), BF16), v((512, 1024), BF16),
        *[v((4, 4, 4, n, 128), BF16) for n in sizes],
        *[v((4, 2, 2, n, 128), BF16) for n in sizes],
        *[v((4, 2, 4, n, 128), BF16) for n in sizes],
        *[v((4, 4, n, 128), BF16) for n in sizes],
        *[v((4, 3, n, 128), BF16) for n in sizes],
        *[v((4, n, 128), BF16) for n in sizes],
        *[v((3, n, 128), BF16) for n in sizes],
        v((3, 128, 512), F32), v((512, 128), F32), v((2, 8, 128), F32), v((7, 8, 128), F32), v((15, 8, 128), F32),
        v((128, 512), F32), v((64, 512), F32), v((4, 128, 128), BF16), v((4, 512, 128), BF16),
        v((16, 128, 128), BF16), v((16, 128, 128), BF16),
        v((32, 512, 128), BF16), v((32, 512, 128), BF16), v((4, 32, 1024), BF16), v((4, 32, 128), BF16), v((512, 512), BF16),
        v((1024, 128), F32), v((256, 128), F32), v((1024, 128), F32), v((1024, 128), F32), v((32, 32, 128), F32), v((32, 32, 128), F32),
        sem((13,)), sem((4,)), sem((4, 4)), sem((4,)), sem((4,)),
        sem((3,)), sem((4, 3)), sem((3,)), sem((4, 3)), sem((3,)), sem((4, 3)), sem((3,)), sem((3,)),
        sem((2,)), sem((2,)), sem((1,)), sem((4,)), sem((4,)), sem((1,)), sem((1,)), sem((1,)), sem((16,)), sem((1,)), sem((1,)), sem((1,)),
    ]


def on_device(
    acts, cotangent, master, moment1, moment2, hidden_in, k_cache, v_cache, k_new, queries, cache_len
):
    place = pl.BlockSpec(memory_space=pl.ANY)
    new_master, out = pl.pallas_call(
        kernel,
        name="update_and_decode",
        out_shape=(pltpu.VMEM((64, 1024), F32), pltpu.VMEM((4, 32, 1024), BF16)),
        in_specs=[pl.BlockSpec(memory_space=pltpu.SMEM)] + [place] * 10,
        out_specs=(pl.BlockSpec(memory_space=pltpu.VMEM), pl.BlockSpec(memory_space=pltpu.VMEM)),
        scratch_shapes=scratch(),
        compiler_params=pltpu.CompilerParams(
            collective_id=0, has_side_effects=True, vmem_limit_bytes=60 * 2**20
        ),
    )(
        cache_len[0], acts, cotangent, master, moment1, moment2, hidden_in.reshape(128, 1024),
        k_cache[0, 0], v_cache[0, 0], k_new[:, 0, 0], queries[:, 0, 0],
    )
    return new_master, out.reshape(4, 1, 1, 32, 1024)


def solution(mesh):
    rows = P(("fsdp", "dp"), None)
    in_specs = (
        rows, rows, rows, rows, rows,
        P(None, "dp", "fsdp", None, None),
        P("dp", "fsdp", None, None, None),
        P("dp", "fsdp", None, None, None),
        P(None, "dp", "fsdp", None, None),
        P(None, "dp", "fsdp", None, None),
        P("dp", None, None),
    )
    out_specs = (rows, P(None, "dp", "fsdp", None, None))
    return jax.shard_map(on_device, mesh=mesh, in_specs=in_specs, out_specs=out_specs, check_vma=False)
```

```python
import functools

import jax
import jax.numpy as jnp
from jax import lax
from jax.experimental import pallas as pl
from jax.experimental.pallas import tpu as pltpu
from jax.sharding import PartitionSpec as P

MESH = pl.DeviceIdType.MESH
F32 = jnp.float32
BF16 = jnp.bfloat16
PARTS = ((0, 176), (176, 176), (352, 160))
NT = (((1,), (1,)), ((), ()))


def coordinates():
    f, d = lax.axis_index("fsdp"), lax.axis_index("dp")
    return ((f // 4) % 4, f % 4, (d // 2) * 2 + f // 16), d % 2


def device(pos, core):
    x, y, z = pos
    return ((z % 2) * 16 + x * 4 + y, (z // 2) * 2 + core)


def shifted(pos, dim, delta):
    return tuple((v + delta) % 4 if i == dim else v for i, v in enumerate(pos))


def kernel(
    lens, acts, cot, master, mom1, mom2, hid, keys, vals, knew, query,
    nm_out, at_out,
    abuf, cbuf, ct, g0, g1, g2, ra0, ra1, ra2, rb0, rb1, rb2, s0, s1, s2, rc0, rc1, rc2, t0, t1, t2, rd0, rd1, rd2,
    ms, gt, nsend, nra, nrb, nmx, nmr, wsend, wbuf, vs, vr,
    kbuf, vbuf, qbuf, knbuf, hbuf, qs, kns, acc, ens, accn, enn,
    loc, asend, arecv, xsend, xrecv, pas, par, pbs, pbr, p2s, p2r, p3s, p3r, nss, nsr, ws, wr, hs, hr, hfs, hfr, vss, vsr, osend, orecv,
):
    pos, core = coordinates()
    x, y, z = pos
    other = 1 - core
    me = device(pos, core)
    sib = device(pos, other)
    gs, ras, rbs, ss, rcs, ts, rds = (
        (g0, g1, g2), (ra0, ra1, ra2), (rb0, rb1, rb2), (s0, s1, s2), (rc0, rc1, rc2), (t0, t1, t2), (rd0, rd1, rd2)
    )

    def copy(src, dst, sem):
        return pltpu.make_async_copy(src, dst, sem)

    def remote(src, dst, ssem, rsem, dev):
        return pltpu.make_async_remote_copy(
            src_ref=src, dst_ref=dst, send_sem=ssem, recv_sem=rsem, device_id=dev, device_id_type=MESH
        )

    def drain(ref, sem):
        pltpu.make_async_copy(ref, ref, sem).wait()

    def lanes(k, j):
        xb, yb = j // 4, j % 4
        zb = (k + 8 - xb - yb) % 4
        return pl.ds(pl.multiple_of((((zb % 2) * 16 + xb * 4 + yb) * 2 + zb // 2) * 128, 128), 128)

    half = pl.ds(pl.multiple_of(core * 512, 512), 512)
    far = pl.ds(pl.multiple_of(other * 512, 512), 512)
    mine = pl.ds(pl.multiple_of(core * 64, 64), 64)
    theirs = pl.ds(pl.multiple_of(other * 64, 64), 64)

    tokens_here = pl.ds(pl.multiple_of(core * 256, 256), 256)
    tokens_there = pl.ds(pl.multiple_of(other * 256, 256), 256)

    def hidden_target(yb):
        src = hid.at[:, pl.ds(pl.multiple_of(yb * 256, 256), 256)]
        dst = hbuf.at[
            pl.ds(pl.multiple_of(core * 256 + (x // 2) * 128, 128), 128),
            pl.ds(pl.multiple_of((x % 2) * 256, 256), 256),
        ]
        return (y, yb, z), src, dst, (y == x) & (yb == y)

    barrier = pltpu.get_barrier_semaphore()
    pl.semaphore_signal(barrier, inc=1, device_id=sib, device_id_type=MESH)
    for dim in (2, 1, 0):
        for delta in (2, 1, 3):
            pl.semaphore_signal(barrier, inc=1, device_id=device(shifted(pos, dim, delta), core), device_id_type=MESH)

    copy(cot.at[:, half], cbuf.at[0], loc.at[4]).start()
    for k in range(4):
        @pl.loop(0, 16)
        def _(j):
            to = pl.ds(pl.multiple_of(j * 128, 128), 128)
            copy(acts.at[:, lanes(k, j)], abuf.at[k, pl.ds(0, 512), to], loc.at[k]).start()

    copy(query, qbuf, loc.at[6]).start()
    copy(knew, knbuf, loc.at[7]).start()
    copy(keys, kbuf, loc.at[8]).start()
    copy(vals, vbuf, loc.at[9]).start()
    for i, ref in enumerate((master, mom1, mom2)):
        copy(ref.at[:, half], ms.at[i, mine], loc.at[10 + i]).start()
    pl.semaphore_wait(barrier, 10)

    remote(cot.at[:, far], cbuf.at[1], xsend.at[0], xrecv.at[0], sib).start()
    for k in range(4):
        @pl.loop(0, 16)
        def _(j):
            to = pl.ds(pl.multiple_of(j * 128, 128), 128)
            remote(acts.at[:, lanes(k, j)], abuf.at[k, pl.ds(512, 512), to], asend.at[k], arecv.at[k, j // 4], sib).start()

    for i, ref in enumerate((master, mom1, mom2)):
        remote(ref.at[:, far], ms.at[i, mine], xsend.at[1 + i], xrecv.at[1 + i], sib).start()

    copy(cot.at[:, half], cbuf.at[0], loc.at[4]).wait()
    ct[:, 0:512] = cbuf[0].T
    drain(cbuf.at[1], xrecv.at[0])
    ct[:, 512:1024] = cbuf[1].T

    def pass_on(k):
        for p in range(3):
            g, ra, rb = gs[p], ras[p], rbs[p]
            up, down = shifted(pos, p, 1), shifted(pos, p, 3)
            drain(ra.at[k], par.at[k, p])

            @pl.loop(0, 2)
            def _(i):
                g[k, up[p], i] = (g[k, up[p], i].astype(F32) + ra[k, 0, i].astype(F32)).astype(BF16)
                g[k, down[p], 2 + i] = (g[k, down[p], 2 + i].astype(F32) + ra[k, 1, i].astype(F32)).astype(BF16)

            remote(g.at[k, up[p], 0:2], rb.at[k, 0, 0:2], pbs.at[p], pbr.at[k, p], device(up, core)).start()
            remote(g.at[k, down[p], 2:4], rb.at[k, 1, 2:4], pbs.at[p], pbr.at[k, p], device(down, core)).start()

    for k in range(4):
        drain(abuf.at[k, pl.ds(0, 512)], loc.at[k])
        @pl.loop(0, 4)
        def _(xb):
            cols = pl.ds(pl.multiple_of(xb * 512, 512), 512)
            drain(abuf.at[k, pl.ds(512, 512), cols], arecv.at[k, xb])
            res = jnp.dot(ct[...], abuf[k, :, cols], preferred_element_type=F32).astype(BF16)
            for yb in range(4):
                zb = (k + 8 - xb - yb) % 4
                piece = res[:, yb * 128 : (yb + 1) * 128]
                g0[k, xb, yb] = piece[0:176]
                g1[k, yb, zb] = piece[176:352]
                g2[k, zb, xb] = piece[352:512]

        for p in range(3):
            g, ra, rb = gs[p], ras[p], rbs[p]
            up, down, opposite = shifted(pos, p, 1), shifted(pos, p, 3), (pos[p] + 2) % 4
            to_up, to_down = device(up, core), device(down, core)
            remote(g.at[k, opposite, 0:2], ra.at[k, 0], pas.at[p], par.at[k, p], to_up).start()
            remote(g.at[k, opposite, 2:4], ra.at[k, 1], pas.at[p], par.at[k, p], to_down).start()
            remote(g.at[k, up[p], 2:4], rb.at[k, 0, 2:4], pbs.at[p], pbr.at[k, p], to_up).start()
            remote(g.at[k, down[p], 0:2], rb.at[k, 1, 0:2], pbs.at[p], pbr.at[k, p], to_down).start()
        if k > 0:
            pass_on(k - 1)


    copy(query, qbuf, loc.at[6]).wait()
    copy(knew, knbuf, loc.at[7]).wait()
    for s in range(4):
        for h in range(8):
            qs[pl.ds(s * 8 + h, 32, stride=32), :] = qbuf[s, :, h * 128 : (h + 1) * 128].astype(F32)
    kns[...] = jnp.zeros_like(kns)
    for s in range(4):
        kns[pl.ds(s, 32, stride=8), :] = knbuf[s].astype(F32)
    copy(keys, kbuf, loc.at[8]).wait()
    copy(vals, vbuf, loc.at[9]).wait()
    replica = (z % 2) * 2 + x // 2
    scale = 128 ** (-0.5)

    def attend(i):
        rows = pl.ds(pl.multiple_of(i * 32, 32), 32)
        qi = qs[rows, :].astype(BF16)
        sc = lax.dot_general(qi, kbuf[i], NT, preferred_element_type=F32) * scale
        slot = lax.broadcasted_iota(jnp.int32, (32, 512), 1)
        sc = jnp.where(slot < lens[replica, i], sc, -1e30)
        kn = kns[pl.ds(pl.multiple_of(i * 8, 8), 8), :].astype(BF16)
        sn = lax.dot_general(qi, kn, NT, preferred_element_type=F32) * scale
        step = lax.broadcasted_iota(jnp.int32, (32, 8), 0) // 8
        sn = jnp.where(lax.broadcasted_iota(jnp.int32, (32, 8), 1) <= step, sn, -1e30)
        top = jnp.maximum(jnp.max(sc, 1, keepdims=True), jnp.max(sn, 1, keepdims=True))
        ec = jnp.exp(sc - top)
        en = jnp.exp(sn - top)
        inv = 1.0 / (jnp.sum(ec, 1, keepdims=True) + jnp.sum(en, 1, keepdims=True))
        out = jnp.dot(ec.astype(BF16), vbuf[i], preferred_element_type=F32)
        acc[rows, :] = out * inv
        ens[rows, 0:8] = en.astype(BF16).astype(F32) * inv

    def attend_rows(first, pairs=4):
        @pl.loop(0, pairs)
        def _(i):
            attend(first + 2 * i)
            attend(first + 2 * i + 1)

    def first_sum(k):
        for p in range(3):
            b = (p + 1) % 3
            drain(rbs[p].at[k], pbr.at[k, p])

            @pl.loop(0, 4)
            def _(i):
                total = gs[p][k, pos[p], i].astype(F32) + rbs[p][k, 0, i].astype(F32) + rbs[p][k, 1, i].astype(F32)
                ss[p][k, i] = total.astype(BF16)

            for delta in (2, 1, 3):
                to = shifted(pos, b, delta)
                remote(
                    ss[p].at[k, to[b]], rcs[p].at[k, delta - 1], p2s.at[p], p2r.at[k, p], device(to, core)
                ).start()

    def second_sum(k):
        for p in range(3):
            b, c = (p + 1) % 3, (p + 2) % 3
            drain(rcs[p].at[k], p2r.at[k, p])
            total = ss[p][k, pos[b]].astype(F32)
            for slot in range(3):
                total += rcs[p][k, slot].astype(F32)
            ts[p][k] = total.astype(BF16)
            target = (k + 8 - pos[p] - pos[b]) % 4
            delta = (target + 4 - pos[c]) % 4

            @pl.when(delta != 0)
            def _():
                remote(
                    ts[p].at[k], rds[p].at[delta - 1], p3s.at[p], p3r.at[p], device(shifted(pos, c, delta), core)
                ).start()

    attend_rows(0, 2)
    pass_on(3)
    attend_rows(4, 2)
    first_sum(0)
    attend_rows(8)
    first_sum(1)
    second_sum(0)
    first_sum(2)
    second_sum(1)
    first_sum(3)
    second_sum(2)
    second_sum(3)

    own = (x + y + z) % 4
    for p, (first, size) in enumerate(PARTS):
        drain(rds[p], p3r.at[p])
        total = ts[p][own].astype(F32)
        for slot in range(3):
            total += rds[p][slot].astype(F32)
        gt[pl.ds(first, size), :] = total

    square = jnp.zeros((8, 128), F32)
    for i in range(64):
        part = gt[pl.ds(i * 8, 8), :]
        square += part * part
    nsend[0] = square
    for q in (5, 4, 3, 7, 2, 6, 1):
        to = device(((x + q // 2) % 4, y, z), (core + q) % 2)
        remote(nsend.at[0], nra.at[q - 1], nss.at[0], nsr.at[0], to).start()
    attend_rows(16, 4)
    drain(nra, nsr.at[0])
    for slot in range(7):
        square += nra[slot]
    nsend[1] = square
    for q in (10, 9, 11, 6, 14, 2, 8, 5, 7, 13, 15, 1, 3, 4, 12):
        to = device((x, (y + q // 4) % 4, (z + q) % 4), core)
        remote(nsend.at[1], nrb.at[q - 1], nss.at[1], nsr.at[1], to).start()
    @pl.loop(0, 4)
    def _(yb):
        to, src, dst, same = hidden_target(yb)

        @pl.when(jnp.logical_not(same))
        def _():
            remote(src, dst, hs.at[yb], hr.at[0], device(to, core)).start()

        @pl.when(same)
        def _():
            copy(src, dst, hr.at[0]).start()

    attend_rows(24, 4)
    for j in range(32):
        accn[j] = acc[pl.ds(j, 32, stride=32), :]
        enn[j] = ens[pl.ds(j, 32, stride=32), :]
    drain(nrb, nsr.at[1])
    for slot in range(15):
        square += nrb[slot]
    gnorm = jnp.sqrt(jnp.sum(square, keepdims=True))
    clip = jnp.minimum(1.0, 1.0 / (gnorm + 1e-06))

    for i in range(3):
        drain(ms.at[i, mine], loc.at[10 + i])
        drain(ms.at[i, theirs], xrecv.at[1 + i])
    place = pl.ds(pl.multiple_of(((z % 2) * 2 + z // 2) * 128, 128), 128)
    for j in range(4):
        cols = slice(j * 128, (j + 1) * 128)
        clipped = gt[pl.ds(j * 128, 128), :].T * clip
        mom = 0.9 * ms[1, :, cols] + 0.1 * clipped
        sec = 0.95 * ms[2, :, cols] + 0.05 * clipped * clipped
        update = mom / (1.0 - 0.9**10) / (jnp.sqrt(sec / (1.0 - 0.95**10)) + 1e-08)
        weights = ms[0, :, cols]
        weights = weights - 0.1 * (update + 0.1 * weights)
        nmx[:, cols] = weights
        wsend[j] = weights.astype(BF16)
        for q in (2, 1, 3):
            to = (x, y, (z + q) % 4)
            remote(wsend.at[j], wbuf.at[j, place], ws.at[0], wr.at[j], device(to, core)).start()
        copy(wsend.at[j], wbuf.at[j, place], wr.at[j]).start()

    drain(hbuf.at[tokens_here], hr.at[0])
    remote(hbuf.at[tokens_here], hbuf.at[tokens_here], hfs.at[0], hfr.at[0], sib).start()
    remote(nmx.at[theirs], nmr, osend.at[0], orecv.at[0], sib).start()
    nm_out[:, half] = nmx[mine, :]
    drain(hbuf.at[tokens_there], hfr.at[0])
    drain(nmr, orecv.at[0])
    nm_out[:, far] = nmr[...]

    number = x * 4 + y
    for j in range(4):
        drain(wbuf.at[j], wr.at[j])
        res = jnp.dot(hbuf[...], wbuf[j], preferred_element_type=F32).astype(BF16)
        for xp in range(2):
            for c in range(2):
                q = j * 4 + xp * 2 + c
                vs[q] = res[c * 256 + xp * 128 : c * 256 + (xp + 1) * 128]
                to = (xp * 2 + core, j, z)
                same = (to[0] == x) & (to[1] == y) & (c == core)

                @pl.when(jnp.logical_not(same))
                def _():
                    remote(vs.at[q], vr.at[number], vss.at[q], vsr.at[0], device(to, c)).start()

                @pl.when(same)
                def _():
                    copy(vs.at[q], vr.at[number], vsr.at[0]).start()

    drain(vr, vsr.at[0])
    total = vr[0].astype(F32)
    for slot in range(1, 16):
        total += vr[slot].astype(F32)
    vnew = (total * (32.0 * 8192 ** (-0.5))).astype(BF16).astype(F32)
    for s in range(4):
        for h in range(8):
            out = accn[s * 8 + h]
            weight = enn[s * 8 + h]
            for t in range(s + 1):
                out += weight[:, t : t + 1] * vnew[t * 32 : (t + 1) * 32]
            at_out[s, :, h * 128 : (h + 1) * 128] = out.astype(BF16)

    drain(cbuf.at[1], xsend.at[0])
    for i in range(3):
        drain(ms.at[i, theirs], xsend.at[1 + i])
    for k in range(4):
        drain(abuf.at[k, pl.ds(512, 512)], asend.at[k])
    for p in range(3):
        drain(ras[p], pas.at[p])
        drain(rbs[p], pbs.at[p])
        drain(rcs[p], p2s.at[p])
        drain(rds[p], p3s.at[p])
    drain(nra, nss.at[0])
    drain(nrb, nss.at[1])

    drain(wbuf.at[:, pl.ds(0, 384)], ws.at[0])

    @pl.loop(0, 16)
    def _(q):
        same = ((q // 2) % 2 * 2 + core == x) & (q // 4 == y) & (q % 2 == core)

        @pl.when(jnp.logical_not(same))
        def _():
            drain(vs.at[q], vss.at[q])

    @pl.loop(0, 4)
    def _(yb):
        _, _, dst, same = hidden_target(yb)

        @pl.when(jnp.logical_not(same))
        def _():
            drain(dst, hs.at[yb])

    drain(nmr, osend.at[0])
    drain(hbuf.at[tokens_here], hfs.at[0])


def scratch():
    v, sem = pltpu.VMEM, pltpu.SemaphoreType.DMA
    sizes = [size for _, size in PARTS]
    return [
        v((4, 1024, 2048), BF16), v((2, 512, 512), BF16), v((512, 1024), BF16),
        *[v((4, 4, 4, n, 128), BF16) for n in sizes],
        *[v((4, 2, 2, n, 128), BF16) for n in sizes],
        *[v((4, 2, 4, n, 128), BF16) for n in sizes],
        *[v((4, 4, n, 128), BF16) for n in sizes],
        *[v((4, 3, n, 128), BF16) for n in sizes],
        *[v((4, n, 128), BF16) for n in sizes],
        *[v((3, n, 128), BF16) for n in sizes],
        v((3, 128, 512), F32), v((512, 128), F32), v((2, 8, 128), F32), v((7, 8, 128), F32), v((15, 8, 128), F32),
        v((128, 512), F32), v((64, 512), F32), v((4, 128, 128), BF16), v((4, 512, 128), BF16),
        v((16, 128, 128), BF16), v((16, 128, 128), BF16),
        v((32, 512, 128), BF16), v((32, 512, 128), BF16), v((4, 32, 1024), BF16), v((4, 32, 128), BF16), v((512, 512), BF16),
        v((1024, 128), F32), v((256, 128), F32), v((1024, 128), F32), v((1024, 128), F32), v((32, 32, 128), F32), v((32, 32, 128), F32),
        sem((13,)), sem((4,)), sem((4, 4)), sem((4,)), sem((4,)),
        sem((3,)), sem((4, 3)), sem((3,)), sem((4, 3)), sem((3,)), sem((4, 3)), sem((3,)), sem((3,)),
        sem((2,)), sem((2,)), sem((1,)), sem((4,)), sem((4,)), sem((1,)), sem((1,)), sem((1,)), sem((16,)), sem((1,)), sem((1,)), sem((1,)),
    ]


def on_device(
    acts, cotangent, master, moment1, moment2, hidden_in, k_cache, v_cache, k_new, queries, cache_len
):
    place = pl.BlockSpec(memory_space=pl.ANY)
    new_master, out = pl.pallas_call(
        kernel,
        name="update_and_decode",
        out_shape=(pltpu.VMEM((64, 1024), F32), pltpu.VMEM((4, 32, 1024), BF16)),
        in_specs=[pl.BlockSpec(memory_space=pltpu.SMEM)] + [place] * 10,
        out_specs=(pl.BlockSpec(memory_space=pltpu.VMEM), pl.BlockSpec(memory_space=pltpu.VMEM)),
        scratch_shapes=scratch(),
        compiler_params=pltpu.CompilerParams(
            collective_id=0, has_side_effects=True, vmem_limit_bytes=60 * 2**20
        ),
    )(
        cache_len[0], acts, cotangent, master, moment1, moment2, hidden_in.reshape(128, 1024),
        k_cache[0, 0], v_cache[0, 0], k_new[:, 0, 0], queries[:, 0, 0],
    )
    return new_master, out.reshape(4, 1, 1, 32, 1024)


def solution(mesh):
    rows = P(("fsdp", "dp"), None)
    in_specs = (
        rows, rows, rows, rows, rows,
        P(None, "dp", "fsdp", None, None),
        P("dp", "fsdp", None, None, None),
        P("dp", "fsdp", None, None, None),
        P(None, "dp", "fsdp", None, None),
        P(None, "dp", "fsdp", None, None),
        P("dp", None, None),
    )
    out_specs = (rows, P(None, "dp", "fsdp", None, None))
    return jax.shard_map(on_device, mesh=mesh, in_specs=in_specs, out_specs=out_specs, check_vma=False)
```
